512 devices in a mesh: section: 8 (over z), seq: 16 (over y, core), dp: 4 (over x).
Axes of the slice: x: 4, y: 8, z: 8, core: 2. Of those that a mesh axis runs over, the one named last changes fastest.
Arguments:
- wave: bfloat16 [4, 16, 40], P('dp', 'seq'), may hold values from -6 to 6
- lengths: int32 [4, 16], P('dp'), may hold values from 10 to 40, as said below
- assign: int32 [4, 16], P('dp'), may hold values from 0 to 15, each once within a row
- conv_weight: bfloat16 [512, 10], replicated, may hold values from -2 to 2
- conv_bias: float32 [512], replicated, may hold values from -3 to 3
- conv_gain: float32 [512], replicated, may hold values from 0.1 to 1.9
- conv_shift: float32 [512], replicated, may hold values from -3 to 3
- feat_gain: float32 [512], replicated, may hold values from 0.1 to 1.9
- feat_shift: float32 [512], replicated, may hold values from -3 to 3
- proj_weight: bfloat16 [512, 4096], P(None, 'seq'), may hold values from -0.25 to 0.25
- proj_bias: float32 [4096], P('seq'), may hold values from -3 to 3
- norm_gain: float32 [8, 4096], P('section'), may hold values from 0.1 to 1.9
- norm_shift: float32 [8, 4096], P('section'), may hold values from -3 to 3
- query_weight: bfloat16 [8, 4096, 2048], P('section', None, 'seq'), may hold values from -1 to 1
- key_weight: bfloat16 [8, 4096, 2048], P('section', None, 'seq'), may hold values from -1 to 1
- value_weight: bfloat16 [8, 4096, 2048], P('section', None, 'seq'), may hold values from -0.09375 to 0.09375
- out_weight: bfloat16 [8, 2048, 4096], P('section', None, 'seq'), may hold values from -0.125 to 0.125
- out_bias: float32 [8, 4096], P('section', 'seq'), may hold values from -3 to 3
- feat_grad: bfloat16 [4, 16, 8, 512], P('dp', 'seq'), may hold values from -0.25 to 0.25
Outputs:
- section_out: bfloat16 [8, 4, 2, 64, 4096], P('section', 'dp', None, None, 'seq')
- conv_weight_grad: float32 [512, 10], replicated
- conv_bias_grad: float32 [512], replicated
- conv_gain_grad: float32 [512], replicated
- conv_shift_grad: float32 [512], replicated
The draws below stay inside these ranges and needn't reach their ends.
Inputs may be any that keep to these rules, and one draw needn't show every extreme that they name: `lengths`: one utterance has length 40 and one has length 10. `assign`: each row holds every number below 16 once.
All inputs are finite; a program needn't handle non-finite values.
Results may differ from the reference program's by a relative error of at most 0.04.
Values may be sent and summed in bfloat16 or wider, within the bound.
No kernel may reach another device: no remote copies, remote signals or barrier semaphores. Data moves between devices by JAX's collectives and lax.ppermute only.
A program may use at most 64 MiB of HBM per device.

```python
import jax
import jax.numpy as jnp
from jax import lax

D = 4096
HEADS = 16
HEAD_DIM = 128
CH = 512
KERNEL = 10
STRIDE = 5
UTT_FRAMES = 8
MICRO = 2
BATCH = 16
UTTS = 8
SAMPLES = 40
ROWS = 64
REPLICAS = 4
SECTIONS = 8


def draw_lengths(key, part):
    key = jax.random.fold_in(key, 7)
    first, second = jax.random.split(key)
    drawn = jax.random.randint(first, (REPLICAS * BATCH,), KERNEL, SAMPLES + 1)
    places = jax.random.permutation(second, REPLICAS * BATCH)
    drawn = drawn.at[places[0]].set(SAMPLES)
    drawn = drawn.at[places[1]].set(KERNEL)
    return drawn.reshape(REPLICAS, BATCH).astype(jnp.int32)


def drawn_parts(key):
    first, second, third = jax.random.split(key, 3)
    along_model = jax.random.truncated_normal(first, -4.0, 4.0, (SECTIONS, HEADS, D), jnp.float32) * D ** (-0.5)
    along_head = jax.random.truncated_normal(second, -4.0, 4.0, (SECTIONS, HEADS, HEAD_DIM), jnp.float32)
    level = jax.random.uniform(third, (SECTIONS, HEADS), jnp.float32)
    return (along_model, along_head, level)


def drawn_weight(key, parts, weakest, strongest):
    along_model, along_head, level = parts
    strength = weakest * (strongest / weakest) ** level
    amplitude = jnp.sqrt(strength) * HEAD_DIM ** (-0.25)
    planted = amplitude[:, :, None, None] * along_model[:, :, :, None] * along_head[:, :, None, :]
    planted = jnp.transpose(planted, (0, 2, 1, 3)).reshape(SECTIONS, D, HEADS * HEAD_DIM)
    base = jax.random.truncated_normal(key, -6.0, 6.0, (SECTIONS, D, HEADS * HEAD_DIM), jnp.float32) * D ** (-0.5)
    return jnp.clip(base + planted, -1.0, 1.0).astype(jnp.bfloat16)


def draw_query_weight(key, part):
    parts = drawn_parts(key)
    key = jax.random.fold_in(key, 11)
    return drawn_weight(key, parts, 0.5, 4.0)


def draw_key_weight(key, part):
    parts = drawn_parts(key)
    key = jax.random.fold_in(key, 13)
    return drawn_weight(key, parts, 0.5, 4.0)


def steps_of(own_key, extent, cuts, smallest, largest):
    level, own = 1.0, jax.random.fold_in(own_key, 6)
    for dim, blocks in cuts:
        draws = jnp.exp(jax.random.uniform(jax.random.fold_in(own, dim), (blocks,), jnp.float32, smallest / len(cuts), largest / len(cuts)))
        level = level * jnp.repeat(draws, extent[dim] // blocks).reshape([-1 if axis == dim else 1 for axis in range(len(extent))])
    return level


def normal_values(rng, extent, width, limit, shards=(), held_as=jnp.bfloat16):
    values = jax.random.normal(rng, extent, jnp.float32) * width
    if len(shards) > 0:
        values = steps_of(rng, extent, shards, -0.22, 0.18) * values
    return jnp.clip(values, min=-limit, max=limit).astype(held_as)


def setup_inputs(seed: int = 0) -> dict:
    key_list = jax.random.split(jax.random.key(seed), 20)
    wave = normal_values(key_list[0], (REPLICAS, BATCH, SAMPLES), 1.0, 6.0, ((0, 4), (1, 16)))
    lengths = draw_lengths(jax.random.fold_in(key_list[19], 71), 0)
    assign = jax.vmap(lambda own: jax.random.permutation(own, BATCH))(jax.random.split(key_list[2], REPLICAS)).reshape((REPLICAS, BATCH)).astype(jnp.int32)
    conv_weight = normal_values(key_list[3], (CH, KERNEL), KERNEL ** -0.5, 2.0)
    conv_bias = normal_values(key_list[4], (CH,), 0.5, 3.0, (), jnp.float32)
    conv_gain = jnp.clip(1.0 + 0.18 * jax.random.normal(key_list[5], (CH,), jnp.float32), 0.1, 1.9)
    conv_shift = normal_values(key_list[6], (CH,), 0.5, 3.0, (), jnp.float32)
    feat_gain = jnp.clip(1.0 + 0.18 * jax.random.normal(key_list[7], (CH,), jnp.float32), 0.1, 1.9)
    feat_shift = normal_values(key_list[8], (CH,), 0.5, 3.0, (), jnp.float32)
    proj_weight = normal_values(key_list[9], (CH, D), CH ** -0.5, 0.25, ((1, 16),))
    proj_bias = normal_values(key_list[10], (D,), 0.5, 3.0, ((0, 16),), jnp.float32)
    norm_gain = jnp.clip(1.0 + 0.18 * jax.random.normal(key_list[11], (SECTIONS, D), jnp.float32), 0.1, 1.9)
    norm_shift = normal_values(key_list[12], (SECTIONS, D), 0.5, 3.0, ((0, 8),), jnp.float32)
    query_weight = draw_query_weight(jax.random.fold_in(key_list[19], 71), 0)
    key_weight = draw_key_weight(jax.random.fold_in(key_list[19], 71), 0)
    value_weight = normal_values(key_list[15], (SECTIONS, D, HEADS * HEAD_DIM), D ** -0.5, 0.09375, ((0, 8), (2, 16)))
    out_weight = normal_values(key_list[16], (SECTIONS, HEADS * HEAD_DIM, D), (HEADS * HEAD_DIM) ** -0.5, 0.125, ((0, 8), (2, 16)))
    out_bias = normal_values(key_list[17], (SECTIONS, D), 0.5, 3.0, ((0, 8), (1, 16)), jnp.float32)
    feat_grad = normal_values(key_list[18], (REPLICAS, BATCH, UTT_FRAMES, CH), (REPLICAS * BATCH * UTT_FRAMES) ** -0.5, 0.25, ((0, 4), (1, 16)))
    return {"wave": wave, "lengths": lengths, "assign": assign, "conv_weight": conv_weight, "conv_bias": conv_bias, "conv_gain": conv_gain, "conv_shift": conv_shift, "feat_gain": feat_gain, "feat_shift": feat_shift, "proj_weight": proj_weight, "proj_bias": proj_bias, "norm_gain": norm_gain, "norm_shift": norm_shift, "query_weight": query_weight, "key_weight": key_weight, "value_weight": value_weight, "out_weight": out_weight, "out_bias": out_bias, "feat_grad": feat_grad}


def layer_norm(values, gain, shift):
    average = lax.optimization_barrier(jnp.mean(values, axis=-1, keepdims=True))
    centered = values - average
    spread = lax.optimization_barrier(jnp.mean(centered * centered, axis=-1, keepdims=True))
    return centered * lax.rsqrt(spread + 1e-05) * gain + shift

def frame_counts(lengths):
    return (lengths - KERNEL) // STRIDE + 1

def frontend(weight, bias, gain, shift, framed, live):
    convolved = jnp.einsum('...fk,ck->...fc', framed, weight, precision=lax.Precision.HIGHEST) + bias
    active = jax.nn.gelu(layer_norm(convolved, gain, shift), approximate=False)
    return jnp.where(live[..., None], active, jnp.zeros_like(active))

def attention_layer(x, counts, gain, shift, query_weight, key_weight, value_weight, out_weight, out_bias):
    batches, row_count, model_width = x.shape
    owners = counts.shape[1]
    frames = row_count // owners
    head_count = query_weight.shape[1] // HEAD_DIM
    flattened = x.reshape(batches * row_count, model_width)
    normed = layer_norm(flattened.astype(jnp.float32), gain, shift).astype(jnp.bfloat16)
    queries = (jnp.dot(normed, query_weight, preferred_element_type=jnp.float32) * HEAD_DIM ** (-0.5)).astype(jnp.bfloat16)
    key_rows = jnp.dot(normed, key_weight, preferred_element_type=jnp.float32).astype(jnp.bfloat16)
    value_rows = jnp.dot(normed, value_weight, preferred_element_type=jnp.float32).astype(jnp.bfloat16)
    split_shape = (batches, owners, frames, head_count, HEAD_DIM)
    scores = jnp.einsum('bufhd,bughd->buhfg', queries.astype(jnp.float32).reshape(split_shape), key_rows.astype(jnp.float32).reshape(split_shape), precision=lax.Precision.HIGHEST)
    is_live = lax.broadcasted_iota(jnp.int32, (batches, owners, frames), 2) < counts[:, :, None]
    scores = jnp.where(is_live[:, :, None, None, :], scores, -jnp.inf)
    row_max = lax.optimization_barrier(jnp.max(scores, axis=-1, keepdims=True))
    raised = jnp.exp(scores - row_max)
    attention = (raised / lax.optimization_barrier(jnp.sum(raised, axis=-1, keepdims=True))).astype(jnp.bfloat16)
    mixture = jnp.einsum('buhfg,bughd->bufhd', attention.astype(jnp.float32), value_rows.astype(jnp.float32).reshape(split_shape), precision=lax.Precision.HIGHEST)
    mixture = mixture.astype(jnp.bfloat16).reshape(batches * row_count, head_count * HEAD_DIM)
    branch = jnp.dot(mixture, out_weight, preferred_element_type=jnp.float32)
    return (flattened.astype(jnp.float32) + branch + out_bias).astype(jnp.bfloat16).reshape(batches, row_count, model_width)

def reference(wave, lengths, assign, conv_weight, conv_bias, conv_gain, conv_shift, feat_gain, feat_shift, proj_weight, proj_bias, norm_gain, norm_shift, query_weight, key_weight, value_weight, out_weight, out_bias, feat_grad):
    positions = lax.broadcasted_iota(jnp.int32, wave.shape, 2)
    cleaned = jnp.where(positions < lengths[:, :, None], wave, jnp.zeros_like(wave))
    blocks = cleaned.reshape(REPLICAS, BATCH, UTT_FRAMES, STRIDE).astype(jnp.float32)
    after = jnp.concatenate([blocks[:, :, 1:], jnp.zeros((REPLICAS, BATCH, 1, STRIDE), jnp.float32)], axis=2)
    framed = jnp.concatenate([blocks, after], axis=3)
    counts = frame_counts(lengths)
    live = lax.broadcasted_iota(jnp.int32, (REPLICAS, BATCH, UTT_FRAMES), 2) < counts[:, :, None]

    def frontend_at(weight, bias, gain, shift):
        return frontend(weight, bias, gain, shift, framed, live)
    features, pullback = jax.vjp(frontend_at, conv_weight.astype(jnp.float32), conv_bias, conv_gain, conv_shift)
    gradients = pullback(feat_grad.astype(jnp.float32))
    slot_ids = lax.broadcasted_iota(jnp.int32, (1, 1, BATCH), 2)
    chosen = assign[:, :, None] == slot_ids
    ordered = lax.optimization_barrier(jnp.sum(jnp.where(chosen[:, :, :, None, None], features[:, :, None], 0.0), axis=1)).astype(jnp.bfloat16)
    slot_counts = lax.optimization_barrier(jnp.sum(jnp.where(chosen, counts[:, :, None], 0), axis=1))
    frames_all = ordered.reshape(REPLICAS * MICRO, ROWS, CH)
    counts_all = slot_counts.reshape(REPLICAS * MICRO, UTTS)
    normed = layer_norm(frames_all.astype(jnp.float32), feat_gain, feat_shift).astype(jnp.bfloat16)
    projected = jnp.dot(normed.reshape(REPLICAS * MICRO * ROWS, CH), proj_weight, preferred_element_type=jnp.float32) + proj_bias
    start_rows = projected.astype(jnp.bfloat16).reshape(REPLICAS * MICRO, ROWS, D)

    def section_step(x, layer):
        gain, shift, query_part, key_part, value_part, out_part, bias_part = layer
        result = attention_layer(x, counts_all, gain, shift, query_part, key_part, value_part, out_part, bias_part)
        return (result, result)
    _, outputs = lax.scan(section_step, start_rows, (norm_gain, norm_shift, query_weight, key_weight, value_weight, out_weight, out_bias))
    section_out = outputs.reshape(SECTIONS, REPLICAS, MICRO, ROWS, D)
    return (section_out, gradients[0], gradients[1], gradients[2], gradients[3])
```

```python
import functools

import jax
import jax.numpy as jnp
from jax import lax
from jax.sharding import Mesh, PartitionSpec as P

HEAD_DIM = 128
KERNEL = 10
STRIDE = 5
MICRO = 2
CORES = 2


def layer_norm(values, gain, shift):
    average = jnp.mean(values, axis=-1, keepdims=True)
    centered = values - average
    spread = jnp.mean(centered * centered, axis=-1, keepdims=True)
    return centered * lax.rsqrt(spread + 1e-05) * gain + shift


def frame_counts(lengths):
    return (lengths - KERNEL) // STRIDE + 1


def framed_of(wave, lengths):
    owners, samples = wave.shape
    positions = lax.broadcasted_iota(jnp.int32, wave.shape, 1)
    cleaned = jnp.where(positions < lengths[:, None], wave, jnp.zeros_like(wave))
    blocks = cleaned.reshape(owners, samples // STRIDE, STRIDE)
    after = jnp.concatenate([blocks[:, 1:], jnp.zeros_like(blocks[:, :1])], axis=1)
    return jnp.concatenate([blocks, after], axis=2)


def live_of(lengths, frame_total):
    counts = frame_counts(lengths)
    return lax.broadcasted_iota(jnp.int32, (lengths.shape[0], frame_total), 1) < counts[:, None]


def frontend(weight, bias, gain, shift, framed, live):
    convolved = (
        jnp.einsum("...fk,ck->...fc", framed, weight, precision=lax.Precision.HIGHEST) + bias
    )
    active = jax.nn.gelu(layer_norm(convolved, gain, shift), approximate=False)
    return jnp.where(live[..., None], active, jnp.zeros_like(active))


def one_head(normed, counts, query_weight, key_weight, value_weight):
    rows = normed.shape[0]
    owners = counts.shape[0]
    frames = rows // owners
    product = functools.partial(jnp.dot, preferred_element_type=jnp.float32)
    queries = (product(normed, query_weight) * HEAD_DIM ** (-0.5)).astype(jnp.bfloat16)
    key_rows = product(normed, key_weight).astype(jnp.bfloat16)
    value_rows = product(normed, value_weight).astype(jnp.bfloat16)
    split = (owners, frames, HEAD_DIM)
    scores = jnp.einsum(
        "ufd,ugd->ufg",
        queries.reshape(split),
        key_rows.reshape(split),
        preferred_element_type=jnp.float32,
    )
    live = lax.broadcasted_iota(jnp.int32, (owners, frames), 1) < counts[:, None]
    scores = jnp.where(live[:, None, :], scores, -jnp.inf)
    raised = jnp.exp(scores - jnp.max(scores, axis=-1, keepdims=True))
    attention = (raised / jnp.sum(raised, axis=-1, keepdims=True)).astype(jnp.bfloat16)
    mixture = jnp.einsum(
        "ufg,ugd->ufd",
        attention,
        value_rows.reshape(split),
        preferred_element_type=jnp.float32,
    )
    return mixture.astype(jnp.bfloat16).reshape(rows, HEAD_DIM)


def on_device(
    wave,
    lengths,
    assign,
    conv_weight,
    conv_bias,
    conv_gain,
    conv_shift,
    feat_gain,
    feat_shift,
    proj_weight,
    proj_bias,
    norm_gain,
    norm_shift,
    query_weight,
    key_weight,
    value_weight,
    out_weight,
    out_bias,
    feat_grad,
):
    section = lax.axis_index("section")
    core = lax.axis_index("core")
    sections = lax.axis_size("section")
    seq_index = lax.axis_index("y") * CORES + core
    samples = wave.shape[2]
    frame_total = samples // STRIDE
    batch_size = lengths.shape[1]
    utts = batch_size // MICRO

    def swapped(value):
        return lax.ppermute(value, "core", [(0, 1), (1, 0)])

    def in_order(mine, others):
        return jnp.where(core == 0, jnp.stack([mine, others]), jnp.stack([others, mine]))

    waves = lax.all_gather(wave[0], ("y", "core"), axis=0, tiled=True)
    proj_other = swapped(proj_weight)
    bias_mine = jnp.stack([proj_bias, out_bias[0]])
    bias_other = swapped(bias_mine)
    query_pair = (query_weight[0], swapped(query_weight[0]))
    key_pair = (key_weight[0], swapped(key_weight[0]))
    value_pair = (value_weight[0], swapped(value_weight[0]))
    out_pair = (out_weight[0], swapped(out_weight[0]))

    slots = core * utts + lax.broadcasted_iota(jnp.int32, (batch_size, utts), 1)
    chosen = assign[0][:, None] == slots
    slot_lengths = jnp.sum(jnp.where(chosen, lengths[0][:, None], 0), axis=0)
    slot_waves = jnp.sum(
        jnp.where(chosen[:, :, None], waves[:, None].astype(jnp.float32), 0.0), axis=0
    ).astype(jnp.bfloat16)
    framed = framed_of(slot_waves, slot_lengths)
    convolved = (
        jnp.einsum("ufk,ck->ufc", framed, conv_weight, preferred_element_type=jnp.float32)
        + conv_bias
    )
    active = jax.nn.gelu(layer_norm(convolved, conv_gain, conv_shift), approximate=False)
    live = live_of(slot_lengths, frame_total)
    frames = jnp.where(live[..., None], active, 0.0).astype(jnp.bfloat16)
    frames = frames.reshape(utts * frame_total, frames.shape[2])
    normed_frames = layer_norm(frames.astype(jnp.float32), feat_gain, feat_shift).astype(
        jnp.bfloat16
    )

    def projected(weight, bias):
        total = jnp.dot(normed_frames, weight, preferred_element_type=jnp.float32)
        return (total + bias).astype(jnp.bfloat16)

    entering = in_order(projected(proj_weight, proj_bias), projected(proj_other, bias_other[0]))
    counts = frame_counts(slot_lengths)

    def attend(current):
        gathered = lax.all_gather(current, "y", axis=0, tiled=False)
        rows = gathered.shape[2]
        whole = gathered.transpose(2, 0, 1, 3).reshape(rows, -1)
        normed = layer_norm(whole.astype(jnp.float32), norm_gain[0], norm_shift[0]).astype(
            jnp.bfloat16
        )
        mine, others = (
            one_head(normed, counts, query_pair[i], key_pair[i], value_pair[i]) for i in range(2)
        )
        mixed = lax.all_gather(in_order(mine, others), "y", axis=0, tiled=False)
        mixed = mixed.transpose(2, 0, 1, 3).reshape(rows, -1)
        branches = in_order(
            jnp.dot(mixed, out_pair[0], preferred_element_type=jnp.float32) + bias_mine[1],
            jnp.dot(mixed, out_pair[1], preferred_element_type=jnp.float32) + bias_other[1],
        )
        return (current.astype(jnp.float32) + branches).astype(jnp.bfloat16)

    def gradients_of():
        own_lengths = lax.dynamic_slice_in_dim(lengths[0], seq_index, 1, 0)
        own_framed = framed_of(wave[0], own_lengths).astype(jnp.float32)
        own_live = live_of(own_lengths, frame_total)

        def frontend_at(weight, bias, gain, shift):
            return frontend(weight, bias, gain, shift, own_framed, own_live)

        _, pullback = jax.vjp(
            frontend_at, conv_weight.astype(jnp.float32), conv_bias, conv_gain, conv_shift
        )
        partial = pullback(feat_grad[0].astype(jnp.float32))
        packed = jnp.concatenate(
            [partial[0].T, partial[1][None], partial[2][None], partial[3][None]], axis=0
        )
        packed = jnp.pad(packed, ((0, 16 - packed.shape[0]), (0, 0)))
        packed = lax.psum(packed, "core")
        packed = lax.psum(packed, "dp")
        return lax.psum(packed, "y")

    early = section >= sections // 2
    packed = lax.cond(
        early, gradients_of, lambda: jnp.zeros((16, conv_bias.shape[0]), jnp.float32)
    )
    entering, packed = lax.optimization_barrier((entering, packed))

    current, result = entering, entering
    for tick in range(sections):
        result = lax.cond(section == tick, lambda now, was: attend(now), lambda now, was: was, current, result)
        if tick < sections - 1:
            current = lax.ppermute(result, "section", [(tick, tick + 1)])

    result, packed = lax.optimization_barrier((result, packed))
    packed = lax.cond(early, lambda: packed, gradients_of)
    mine = lax.dynamic_index_in_dim(result, core, 0, keepdims=False)
    leaving = lax.dynamic_index_in_dim(result, 1 - core, 0, keepdims=False)
    section_out = in_order(mine, swapped(leaving))[None, None]
    return (section_out, packed[:KERNEL].T, packed[KERNEL], packed[KERNEL + 1], packed[KERNEL + 2])


def solution(mesh):
    sizes = dict(mesh.shape)
    split = Mesh(
        mesh.devices.reshape(
            sizes["section"], sizes["seq"] // CORES, CORES, sizes["dp"]
        ),
        ("section", "y", "core", "dp"),
    )
    seq = ("y", "core")
    return jax.shard_map(
        on_device,
        mesh=split,
        in_specs=(
            P("dp", seq, None),
            P("dp", None),
            P("dp", None),
            P(),
            P(),
            P(),
            P(),
            P(),
            P(),
            P(None, seq),
            P(seq),
            P("section", None),
            P("section", None),
            P("section", None, seq),
            P("section", None, seq),
            P("section", None, seq),
            P("section", None, seq),
            P("section", seq),
            P("dp", seq, None, None),
        ),
        out_specs=(P("section", "dp", None, None, seq), P(), P(), P(), P()),
        check_vma=False,
    )
```

```python
import functools

import jax
import jax.numpy as jnp
from jax import lax
from jax.experimental import pallas as pl
from jax.experimental.pallas import tpu as pltpu
from jax.sharding import Mesh, PartitionSpec as P

HEAD_DIM = 128
KERNEL = 10
STRIDE = 5
MICRO = 2
CORES = 2
LANES = 128


def layer_norm(values, gain, shift):
    average = jnp.mean(values, axis=-1, keepdims=True)
    centered = values - average
    spread = jnp.mean(centered * centered, axis=-1, keepdims=True)
    return centered * lax.rsqrt(spread + 1e-05) * gain + shift


def frame_counts(lengths):
    return (lengths - KERNEL) // STRIDE + 1


def framed_of(wave, lengths):
    owners, samples = wave.shape
    positions = lax.broadcasted_iota(jnp.int32, wave.shape, 1)
    cleaned = jnp.where(positions < lengths[:, None], wave, jnp.zeros_like(wave))
    blocks = cleaned.reshape(owners, samples // STRIDE, STRIDE)
    after = jnp.concatenate([blocks[:, 1:], jnp.zeros_like(blocks[:, :1])], axis=1)
    return jnp.concatenate([blocks, after], axis=2)


def live_of(lengths, frame_total):
    counts = frame_counts(lengths)
    return lax.broadcasted_iota(jnp.int32, (lengths.shape[0], frame_total), 1) < counts[:, None]


def frontend(weight, bias, gain, shift, framed, live):
    convolved = (
        jnp.einsum("...fk,ck->...fc", framed, weight, precision=lax.Precision.HIGHEST) + bias
    )
    active = jax.nn.gelu(layer_norm(convolved, gain, shift), approximate=False)
    return jnp.where(live[..., None], active, jnp.zeros_like(active))


def product(left, right):
    return jnp.dot(left, right, preferred_element_type=jnp.float32)


def mixing_kernel(chips, place, *refs):
    blocks = refs[:chips]
    gain, shift, weights_mine, weights_other, masking, out, held, sems = refs[chips:]
    chip, core = place[0], place[1]
    order = [lax.rem(chip - j + chips, chips) for j in range(chips)]
    copies = []
    for j in range(chips):
        for side, weights in enumerate((weights_mine, weights_other)):
            copy = pltpu.make_async_copy(
                weights.at[order[j], 0:3], held.at[j, side], sems.at[j, side]
            )
            copy.start()
            copies.append(copy)
    rows, width = blocks[0].shape
    total = sum(jnp.sum(b[...].astype(jnp.float32), axis=-1, keepdims=True) for b in blocks)
    average = total / (chips * width)
    spread = jnp.zeros_like(average)
    for b in blocks:
        centered = b[...].astype(jnp.float32) - average
        spread += jnp.sum(centered * centered, axis=-1, keepdims=True)
    scale = lax.rsqrt(spread / (chips * width) + 1e-05)
    sums = [jnp.zeros((rows, 2 * HEAD_DIM), jnp.float32) for _ in range(3)]
    for j in range(chips):
        centered = blocks[j][...].astype(jnp.float32) - average
        normed = (centered * scale * gain[order[j]] + shift[order[j]]).astype(jnp.bfloat16)
        copies[2 * j].wait()
        copies[2 * j + 1].wait()
        for i in range(3):
            both = jnp.concatenate([held[j, 0, i], held[j, 1, i]], axis=1)
            sums[i] += product(normed, both)
    queries = (sums[0] * HEAD_DIM ** (-0.5)).astype(jnp.bfloat16)
    key_rows = sums[1].astype(jnp.bfloat16)
    value_rows = sums[2].astype(jnp.bfloat16)
    for side in range(2):
        own = slice(side * HEAD_DIM, (side + 1) * HEAD_DIM)
        scores = lax.dot_general(
            queries[:, own],
            key_rows[:, own],
            (((1,), (1,)), ((), ())),
            preferred_element_type=jnp.float32,
        )
        scores = jnp.where(masking[...] > 0, scores, -jnp.inf)
        raised = jnp.exp(scores - jnp.max(scores, axis=-1, keepdims=True))
        attention = (raised / jnp.sum(raised, axis=-1, keepdims=True)).astype(jnp.bfloat16)
        mixture = product(attention, value_rows[:, own]).astype(jnp.bfloat16)
        lane = pl.multiple_of((core if side == 0 else 1 - core) * HEAD_DIM, HEAD_DIM)
        out[:, pl.ds(lane, HEAD_DIM)] = mixture


def leaving_kernel(chips, place, mixed, current, weights_mine, weights_other, bias, out, held, sems):
    core = place[1]
    copies = []
    for side, weights in enumerate((weights_mine, weights_other)):
        for i in range(chips):
            copy = pltpu.make_async_copy(weights.at[i, 3], held.at[side, i], sems.at[side, i])
            copy.start()
            copies.append(copy)
    depth = mixed.shape[2]
    columns = 2 * LANES
    for side in range(2):
        total = jnp.zeros((mixed.shape[1], columns), jnp.float32)
        for i in range(chips):
            copies[side * chips + i].wait()
            both = jnp.concatenate([held[side, i, :depth], held[side, i, depth:]], axis=1)
            total += product(mixed[i], both)
        lane = pl.multiple_of((core if side == 0 else 1 - core) * columns, columns)
        mine = pl.ds(lane, columns)
        out[:, mine] = (current[:, mine].astype(jnp.float32) + total + bias[:, mine]).astype(
            jnp.bfloat16
        )


def on_device(
    wave,
    lengths,
    assign,
    conv_weight,
    conv_bias,
    conv_gain,
    conv_shift,
    feat_gain,
    feat_shift,
    proj_weight,
    proj_bias,
    norm_gain,
    norm_shift,
    query_weight,
    key_weight,
    value_weight,
    out_weight,
    out_bias,
    feat_grad,
):
    section, chip, core = (lax.axis_index(name) for name in ("section", "y", "core"))
    sections, chips = lax.axis_size("section"), lax.axis_size("y")
    samples = wave.shape[2]
    frame_total = samples // STRIDE
    batch_size = lengths.shape[1]
    utts = batch_size // MICRO
    rows = utts * frame_total
    width = query_weight.shape[1] // chips
    columns = proj_weight.shape[1]
    vmem, smem, anywhere = (
        pl.BlockSpec(memory_space=space) for space in (pltpu.VMEM, pltpu.SMEM, pl.ANY)
    )

    def swapped(value):
        return lax.ppermute(value, "core", [(0, 1), (1, 0)])

    depth = out_weight.shape[1] // chips
    halves = out_weight[0].reshape(chips, depth, 2, LANES).transpose(0, 2, 1, 3)
    weights_mine = jnp.stack(
        [
            query_weight[0].reshape(chips, width, HEAD_DIM),
            key_weight[0].reshape(chips, width, HEAD_DIM),
            value_weight[0].reshape(chips, width, HEAD_DIM),
            halves.reshape(chips, width, LANES),
        ],
        axis=1,
    )
    weights_other = swapped(weights_mine)
    proj_other = swapped(proj_weight)

    small = jnp.concatenate([wave[0].astype(jnp.float32), proj_bias[None], out_bias], axis=1)
    small = lax.all_gather(small, ("y", "core"), axis=0, tiled=True)
    waves = small[:, :samples]
    pair = lax.dynamic_slice_in_dim(small, chip * CORES, CORES, 0)
    proj_bias_pair = pair[:, samples : samples + columns].reshape(1, CORES * columns)
    out_bias_pair = pair[:, samples + columns :].reshape(1, CORES * columns)

    slots = core * utts + lax.broadcasted_iota(jnp.int32, (batch_size, utts), 1)
    chosen = assign[0][:, None] == slots
    slot_lengths = jnp.sum(jnp.where(chosen, lengths[0][:, None], 0), axis=0)
    slot_waves = jnp.sum(jnp.where(chosen[:, :, None], waves[:, None], 0.0), axis=0)
    framed = framed_of(slot_waves.astype(jnp.bfloat16), slot_lengths)
    convolved = (
        jnp.einsum("ufk,ck->ufc", framed, conv_weight, preferred_element_type=jnp.float32)
        + conv_bias
    )
    active = jax.nn.gelu(layer_norm(convolved, conv_gain, conv_shift), approximate=False)
    live = live_of(slot_lengths, frame_total)
    frames = jnp.where(live[..., None], active, 0.0).astype(jnp.bfloat16)
    frames = frames.reshape(rows, frames.shape[2])
    normed_frames = layer_norm(frames.astype(jnp.float32), feat_gain, feat_shift).astype(
        jnp.bfloat16
    )
    proj_mine, proj_theirs = product(normed_frames, proj_weight), product(normed_frames, proj_other)
    entering = (
        jnp.where(
            core == 0,
            jnp.concatenate([proj_mine, proj_theirs], axis=1),
            jnp.concatenate([proj_theirs, proj_mine], axis=1),
        )
        + proj_bias_pair
    ).astype(jnp.bfloat16)

    owner = lax.broadcasted_iota(jnp.int32, (rows, rows), 0) // frame_total
    column = lax.broadcasted_iota(jnp.int32, (rows, rows), 1)
    live_keys = live.reshape(1, rows)
    masking = jnp.where((owner == column // frame_total) & live_keys, 1.0, 0.0)
    place = jnp.stack([chip, core]).astype(jnp.int32)
    gain = norm_gain.reshape(chips, 1, width)
    shift = norm_shift.reshape(chips, 1, width)

    def spread_out(block, pairs_of):
        return tuple(
            lax.ppermute(
                block,
                ("section", "y"),
                [
                    (source * chips + y, target * chips + (y + j) % chips)
                    for source, target in pairs_of
                    for y in range(chips)
                ],
            )
            for j in range(chips)
        )

    mixing = pl.pallas_call(
        functools.partial(mixing_kernel, chips),
        out_shape=jax.ShapeDtypeStruct((rows, 2 * HEAD_DIM), jnp.bfloat16),
        in_specs=[smem] + [vmem] * (chips + 2) + [anywhere] * 2 + [vmem],
        out_specs=vmem,
        scratch_shapes=[
            pltpu.VMEM((chips, 2, 3, width, HEAD_DIM), jnp.bfloat16),
            pltpu.SemaphoreType.DMA((chips, 2)),
        ],
        compiler_params=pltpu.CompilerParams(vmem_limit_bytes=24 * 2**20),
    )
    leaving = pl.pallas_call(
        functools.partial(leaving_kernel, chips),
        out_shape=jax.ShapeDtypeStruct((rows, CORES * columns), jnp.bfloat16),
        in_specs=[smem, vmem, vmem, anywhere, anywhere, vmem],
        out_specs=vmem,
        scratch_shapes=[
            pltpu.VMEM((2, chips, width, LANES), jnp.bfloat16),
            pltpu.SemaphoreType.DMA((2, chips)),
        ],
        compiler_params=pltpu.CompilerParams(vmem_limit_bytes=24 * 2**20),
    )

    def attend(received, _):
        mixture = mixing(place, *received, gain, shift, weights_mine, weights_other, masking)
        mixed = lax.all_gather(mixture, "y", axis=0, tiled=False)
        return leaving(place, mixed, received[0], weights_mine, weights_other, out_bias_pair)

    def gradients_of():
        own_lengths = lax.dynamic_slice_in_dim(lengths[0], chip * CORES + core, 1, 0)
        own_framed = framed_of(wave[0], own_lengths).astype(jnp.float32)
        own_live = live_of(own_lengths, frame_total)

        def frontend_at(weight, bias, gain, shift):
            return frontend(weight, bias, gain, shift, own_framed, own_live)

        _, pullback = jax.vjp(
            frontend_at, conv_weight.astype(jnp.float32), conv_bias, conv_gain, conv_shift
        )
        partial = pullback(feat_grad[0].astype(jnp.float32))
        packed = jnp.concatenate(
            [partial[0].T, partial[1][None], partial[2][None], partial[3][None]], axis=0
        )
        packed = jnp.pad(packed, ((0, 16 - packed.shape[0]), (0, 0)))
        return lax.psum(lax.psum(lax.psum(packed, "core"), "dp"), "y")

    late = section >= sections // 2
    packed = lax.cond(
        late, gradients_of, lambda: jnp.zeros((16, conv_bias.shape[0]), jnp.float32)
    )
    entering, packed = lax.optimization_barrier((entering, packed))

    received = spread_out(entering, [(0, 0)])
    result = entering
    for tick in range(sections):
        result = lax.cond(section == tick, attend, lambda now, was: was, received, result)
        if tick < sections - 1:
            received = spread_out(result, [(tick, tick + 1)])

    result, packed = lax.optimization_barrier((result, packed))
    packed = lax.cond(late, lambda: packed, gradients_of)
    mine = lax.dynamic_slice_in_dim(result, core * columns, columns, 1)
    others = swapped(lax.dynamic_slice_in_dim(result, (1 - core) * columns, columns, 1))
    section_out = jnp.where(core == 0, jnp.stack([mine, others]), jnp.stack([others, mine]))
    return (
        section_out[None, None],
        packed[:KERNEL].T,
        packed[KERNEL],
        packed[KERNEL + 1],
        packed[KERNEL + 2],
    )


def solution(mesh):
    sizes = dict(mesh.shape)
    split = Mesh(
        mesh.devices.reshape(
            sizes["section"], sizes["seq"] // CORES, CORES, sizes["dp"]
        ),
        ("section", "y", "core", "dp"),
    )
    seq = ("y", "core")
    return jax.shard_map(
        on_device,
        mesh=split,
        in_specs=(
            P("dp", seq, None),
            P("dp", None),
            P("dp", None),
            P(),
            P(),
            P(),
            P(),
            P(),
            P(),
            P(None, seq),
            P(seq),
            P("section", None),
            P("section", None),
            P("section", None, seq),
            P("section", None, seq),
            P("section", None, seq),
            P("section", None, seq),
            P("section", seq),
            P("dp", seq, None, None),
        ),
        out_specs=(P("section", "dp", None, None, seq), P(), P(), P(), P()),
        check_vma=False,
    )
```

```python
import jax
import jax.numpy as jnp
from jax import lax
from jax.experimental import pallas as pl
from jax.experimental.pallas import tpu as pltpu
from jax.sharding import Mesh, PartitionSpec as P

HEAD_DIM = 128
KERNEL = 10
STRIDE = 5
MICRO = 2
CORES = 2


def layer_norm(values, gain, shift):
    average = jnp.mean(values, axis=-1, keepdims=True)
    centered = values - average
    spread = jnp.mean(centered * centered, axis=-1, keepdims=True)
    return centered * lax.rsqrt(spread + 1e-05) * gain + shift


def frame_counts(lengths):
    return (lengths - KERNEL) // STRIDE + 1


def framed_of(wave, lengths):
    owners, samples = wave.shape
    positions = lax.broadcasted_iota(jnp.int32, wave.shape, 1)
    cleaned = jnp.where(positions < lengths[:, None], wave, jnp.zeros_like(wave))
    blocks = cleaned.reshape(owners, samples // STRIDE, STRIDE)
    after = jnp.concatenate([blocks[:, 1:], jnp.zeros_like(blocks[:, :1])], axis=1)
    return jnp.concatenate([blocks, after], axis=2)


def live_of(lengths, frame_total):
    counts = frame_counts(lengths)
    return lax.broadcasted_iota(jnp.int32, (lengths.shape[0], frame_total), 1) < counts[:, None]


def frontend(weight, bias, gain, shift, framed, live):
    convolved = (
        jnp.einsum("...fk,ck->...fc", framed, weight, precision=lax.Precision.HIGHEST) + bias
    )
    active = jax.nn.gelu(layer_norm(convolved, gain, shift), approximate=False)
    return jnp.where(live[..., None], active, jnp.zeros_like(active))


def product(left, right):
    return jnp.dot(left, right, preferred_element_type=jnp.float32)


def mixing_kernel(blocks, gain, shift, query, key, value, masking, out):
    parts, rows, width = blocks.shape
    total = jnp.zeros((rows, 1), jnp.float32)
    for i in range(parts):
        total += jnp.sum(blocks[i].astype(jnp.float32), axis=-1, keepdims=True)
    average = total / (parts * width)
    spread = jnp.zeros_like(average)
    for i in range(parts):
        centered = blocks[i].astype(jnp.float32) - average
        spread += jnp.sum(centered * centered, axis=-1, keepdims=True)
    scale = lax.rsqrt(spread / (parts * width) + 1e-05)
    both = jnp.zeros((rows, 2 * HEAD_DIM), jnp.float32)
    values = jnp.zeros((rows, HEAD_DIM), jnp.float32)
    for i in range(parts):
        centered = blocks[i].astype(jnp.float32) - average
        normed = (centered * scale * gain[i] + shift[i]).astype(jnp.bfloat16)
        both += product(normed, jnp.concatenate([query[i], key[i]], axis=1))
        values += product(normed, value[i])
    queries = (both[:, :HEAD_DIM] * HEAD_DIM ** (-0.5)).astype(jnp.bfloat16)
    key_rows = both[:, HEAD_DIM:].astype(jnp.bfloat16)
    scores = lax.dot_general(
        queries, key_rows, (((1,), (1,)), ((), ())), preferred_element_type=jnp.float32
    )
    scores = jnp.where(masking[...] > 0, scores, -jnp.inf)
    raised = jnp.exp(scores - jnp.max(scores, axis=-1, keepdims=True))
    attention = (raised / jnp.sum(raised, axis=-1, keepdims=True)).astype(jnp.bfloat16)
    out[...] = product(attention, values.astype(jnp.bfloat16)).astype(jnp.bfloat16)


def leaving_kernel(mixed, current, weights, bias, out):
    total = current[...].astype(jnp.float32) + bias[...]
    for i in range(0, mixed.shape[0], 2):
        pair = jnp.concatenate([mixed[i], mixed[i + 1]], axis=1)
        total += product(pair, weights[i // 2])
    out[...] = total.astype(jnp.bfloat16)


def on_device(
    wave,
    lengths,
    assign,
    conv_weight,
    conv_bias,
    conv_gain,
    conv_shift,
    feat_gain,
    feat_shift,
    proj_weight,
    proj_bias,
    norm_gain,
    norm_shift,
    query_weight,
    key_weight,
    value_weight,
    out_weight,
    out_bias,
    feat_grad,
):
    section, chip, core = (lax.axis_index(name) for name in ("section", "y", "core"))
    sections, chips = lax.axis_size("section"), lax.axis_size("y")
    group = chips * CORES
    samples = wave.shape[2]
    frame_total = samples // STRIDE
    batch_size = lengths.shape[1]
    utts = batch_size // MICRO
    rows = utts * frame_total
    columns = proj_weight.shape[1]

    waves = lax.all_gather(wave[0].astype(jnp.float32), ("y", "core"), axis=0, tiled=True)
    slots = lax.broadcasted_iota(jnp.int32, (batch_size, batch_size), 1)
    chosen = assign[0][:, None] == slots
    slot_lengths = jnp.sum(jnp.where(chosen, lengths[0][:, None], 0), axis=0)
    slot_waves = jnp.sum(jnp.where(chosen[:, :, None], waves[:, None], 0.0), axis=0)
    framed = framed_of(slot_waves.astype(jnp.bfloat16), slot_lengths)
    convolved = (
        jnp.einsum("ufk,ck->ufc", framed, conv_weight, preferred_element_type=jnp.float32)
        + conv_bias
    )
    active = jax.nn.gelu(layer_norm(convolved, conv_gain, conv_shift), approximate=False)
    live = live_of(slot_lengths, frame_total)
    frames = jnp.where(live[..., None], active, 0.0).astype(jnp.bfloat16)
    frames = frames.reshape(MICRO * rows, frames.shape[2])
    normed_frames = layer_norm(frames.astype(jnp.float32), feat_gain, feat_shift).astype(
        jnp.bfloat16
    )
    entering = (product(normed_frames, proj_weight) + proj_bias).astype(jnp.bfloat16)
    entering = entering.reshape(MICRO, rows, columns)

    owner = lax.broadcasted_iota(jnp.int32, (rows, rows), 0) // frame_total
    column = lax.broadcasted_iota(jnp.int32, (rows, rows), 1) // frame_total
    maskings = jnp.where((owner == column)[None] & live.reshape(MICRO, 1, rows), 1.0, 0.0)
    gain = norm_gain.reshape(group, 1, columns)
    shift = norm_shift.reshape(group, 1, columns)
    query, key, value = (
        weight.reshape(group, columns, HEAD_DIM)
        for weight in (query_weight, key_weight, value_weight)
    )
    out_part = out_weight.reshape(group // 2, 2 * HEAD_DIM, columns)

    vmem = pl.BlockSpec(memory_space=pltpu.VMEM)
    mixing = pl.pallas_call(
        mixing_kernel,
        out_shape=jax.ShapeDtypeStruct((rows, HEAD_DIM), jnp.bfloat16),
        in_specs=[vmem] * 7,
        out_specs=vmem,
        compiler_params=pltpu.CompilerParams(vmem_limit_bytes=24 * 2**20),
    )
    leaving = pl.pallas_call(
        leaving_kernel,
        out_shape=jax.ShapeDtypeStruct((rows, columns), jnp.bfloat16),
        in_specs=[vmem] * 4,
        out_specs=vmem,
        compiler_params=pltpu.CompilerParams(vmem_limit_bytes=24 * 2**20),
    )

    def to_all(block, axes, size):
        copies = jnp.broadcast_to(block[None], (size,) + block.shape)
        return lax.all_to_all(copies, axes, 0, 0, tiled=True)

    def attend(current, masking):
        chip_blocks = to_all(current, "y", chips)
        blocks = lax.all_gather(chip_blocks, "core", axis=1, tiled=False)
        blocks = blocks.reshape(group, rows, columns)
        mixture = mixing(blocks, gain, shift, query, key, value, masking)
        mixed = to_all(mixture, ("y", "core"), group)
        return leaving(mixed, current, out_part, out_bias)

    def partial_gradients():
        own_lengths = lax.dynamic_slice_in_dim(lengths[0], chip * CORES + core, 1, 0)
        own_framed = framed_of(wave[0], own_lengths).astype(jnp.float32)
        own_live = live_of(own_lengths, frame_total)

        def frontend_at(weight, bias, gain, shift):
            return frontend(weight, bias, gain, shift, own_framed, own_live)

        _, pullback = jax.vjp(
            frontend_at, conv_weight.astype(jnp.float32), conv_bias, conv_gain, conv_shift
        )
        partial = pullback(feat_grad[0].astype(jnp.float32))
        packed = jnp.concatenate(
            [partial[0].T, partial[1][None], partial[2][None], partial[3][None]], axis=0
        )
        packed = jnp.pad(packed, ((0, 16 - packed.shape[0]), (0, 0)))
        return lax.psum(lax.psum(packed, "core"), "dp")

    gradient_tick = jnp.where(section >= sections // 2, 1, sections - 2)
    ticks = sections + MICRO - 1

    def advance(tick, state):
        previous, outputs, packed = state
        arrived = lax.ppermute(previous, "section", [(s, s + 1) for s in range(sections - 1)])
        piece = tick - section
        slot = jnp.clip(piece, 0, MICRO - 1)
        fresh = lax.dynamic_index_in_dim(entering, slot, 0, keepdims=False)
        current = jnp.where(section == 0, fresh, arrived)
        masking = lax.dynamic_index_in_dim(maskings, slot, 0, keepdims=False)
        kind = jnp.clip(tick - gradient_tick, -1, 2)
        kind = jnp.where((kind == 0) | (kind == 1), kind + 1, 0)
        result, packed = lax.switch(
            kind,
            [
                lambda: (attend(current, masking), packed),
                lambda: (current, partial_gradients()),
                lambda: (current, lax.psum(packed, "y")),
            ],
        )
        kept = lax.dynamic_index_in_dim(outputs, slot, 0, keepdims=False)
        has_work = (piece >= 0) & (piece < MICRO)
        outputs = lax.dynamic_update_index_in_dim(
            outputs, jnp.where(has_work, result, kept), slot, 0
        )
        return (result, outputs, packed)

    start = (
        jnp.zeros((rows, columns), jnp.bfloat16),
        jnp.zeros((MICRO, rows, columns), jnp.bfloat16),
        jnp.zeros((16, conv_bias.shape[0]), jnp.float32),
    )
    _, outputs, packed = lax.fori_loop(0, ticks, advance, start)
    return (
        outputs[None, None],
        packed[:KERNEL].T,
        packed[KERNEL],
        packed[KERNEL + 1],
        packed[KERNEL + 2],
    )


def solution(mesh):
    sizes = dict(mesh.shape)
    split = Mesh(
        mesh.devices.reshape(
            sizes["section"], sizes["seq"] // CORES, CORES, sizes["dp"]
        ),
        ("section", "y", "core", "dp"),
    )
    seq = ("y", "core")
    return jax.shard_map(
        on_device,
        mesh=split,
        in_specs=(
            P("dp", seq, None),
            P("dp", None),
            P("dp", None),
            P(),
            P(),
            P(),
            P(),
            P(),
            P(),
            P(None, seq),
            P(seq),
            P("section", None),
            P("section", None),
            P("section", None, seq),
            P("section", None, seq),
            P("section", None, seq),
            P("section", None, seq),
            P("section", seq),
            P("dp", seq, None, None),
        ),
        out_specs=(P("section", "dp", None, None, seq), P(), P(), P(), P()),
        check_vma=False,
    )
```

```python
import jax
import jax.numpy as jnp
from jax import lax
from jax.experimental import pallas as pl
from jax.experimental.pallas import tpu as pltpu
from jax.sharding import Mesh, PartitionSpec as P

HEAD_DIM = 128
KERNEL = 10
STRIDE = 5
MICRO = 2
CORES = 2


def layer_norm(values, gain, shift):
    average = jnp.mean(values, axis=-1, keepdims=True)
    centered = values - average
    spread = jnp.mean(centered * centered, axis=-1, keepdims=True)
    return centered * lax.rsqrt(spread + 1e-05) * gain + shift


def frame_counts(lengths):
    return (lengths - KERNEL) // STRIDE + 1


def framed_of(wave, lengths):
    owners, samples = wave.shape
    positions = lax.broadcasted_iota(jnp.int32, wave.shape, 1)
    cleaned = jnp.where(positions < lengths[:, None], wave, jnp.zeros_like(wave))
    blocks = cleaned.reshape(owners, samples // STRIDE, STRIDE)
    after = jnp.concatenate([blocks[:, 1:], jnp.zeros_like(blocks[:, :1])], axis=1)
    return jnp.concatenate([blocks, after], axis=2)


def live_of(lengths, frame_total):
    counts = frame_counts(lengths)
    return lax.broadcasted_iota(jnp.int32, (lengths.shape[0], frame_total), 1) < counts[:, None]


def frontend(weight, bias, gain, shift, framed, live):
    convolved = (
        jnp.einsum("...fk,ck->...fc", framed, weight, precision=lax.Precision.HIGHEST) + bias
    )
    active = jax.nn.gelu(layer_norm(convolved, gain, shift), approximate=False)
    return jnp.where(live[..., None], active, jnp.zeros_like(active))


def product(left, right):
    return jnp.dot(left, right, preferred_element_type=jnp.float32)


def mixing_kernel(blocks, gain, shift, query, key, value, masking, out):
    parts, rows, width = blocks.shape
    total = jnp.zeros((rows, 1), jnp.float32)
    for i in range(parts):
        total += jnp.sum(blocks[i].astype(jnp.float32), axis=-1, keepdims=True)
    average = total / (parts * width)
    spread = jnp.zeros_like(average)
    for i in range(parts):
        centered = blocks[i].astype(jnp.float32) - average
        spread += jnp.sum(centered * centered, axis=-1, keepdims=True)
    scale = lax.rsqrt(spread / (parts * width) + 1e-05)
    both = jnp.zeros((rows, 2 * HEAD_DIM), jnp.float32)
    values = jnp.zeros((rows, HEAD_DIM), jnp.float32)
    for i in range(parts):
        centered = blocks[i].astype(jnp.float32) - average
        normed = (centered * scale * gain[i] + shift[i]).astype(jnp.bfloat16)
        both += product(normed, jnp.concatenate([query[i], key[i]], axis=1))
        values += product(normed, value[i])
    queries = (both[:, :HEAD_DIM] * HEAD_DIM ** (-0.5)).astype(jnp.bfloat16)
    key_rows = both[:, HEAD_DIM:].astype(jnp.bfloat16)
    scores = lax.dot_general(
        queries, key_rows, (((1,), (1,)), ((), ())), preferred_element_type=jnp.float32
    )
    scores = jnp.where(masking[...] > 0, scores, -jnp.inf)
    raised = jnp.exp(scores - jnp.max(scores, axis=-1, keepdims=True))
    attention = (raised / jnp.sum(raised, axis=-1, keepdims=True)).astype(jnp.bfloat16)
    out[...] = product(attention, values.astype(jnp.bfloat16)).astype(jnp.bfloat16)


def leaving_kernel(mixed, current, weights, bias, out):
    total = current[...].astype(jnp.float32) + bias[...]
    for i in range(0, mixed.shape[0], 2):
        pair = jnp.concatenate([mixed[i], mixed[i + 1]], axis=1)
        total += product(pair, weights[i // 2])
    out[...] = total.astype(jnp.bfloat16)


def on_device(
    wave,
    lengths,
    assign,
    conv_weight,
    conv_bias,
    conv_gain,
    conv_shift,
    feat_gain,
    feat_shift,
    proj_weight,
    proj_bias,
    norm_gain,
    norm_shift,
    query_weight,
    key_weight,
    value_weight,
    out_weight,
    out_bias,
    feat_grad,
):
    section, chip, core = (lax.axis_index(name) for name in ("section", "y", "core"))
    sections, chips = lax.axis_size("section"), lax.axis_size("y")
    group = chips * CORES
    samples = wave.shape[2]
    frame_total = samples // STRIDE
    batch_size = lengths.shape[1]
    utts = batch_size // MICRO
    rows = utts * frame_total
    columns = proj_weight.shape[1]

    waves = lax.all_gather(wave[0].astype(jnp.float32), ("y", "core"), axis=0, tiled=True)
    slots = lax.broadcasted_iota(jnp.int32, (batch_size, batch_size), 1)
    chosen = assign[0][:, None] == slots
    slot_lengths = jnp.sum(jnp.where(chosen, lengths[0][:, None], 0), axis=0)
    slot_waves = jnp.sum(jnp.where(chosen[:, :, None], waves[:, None], 0.0), axis=0)
    framed = framed_of(slot_waves.astype(jnp.bfloat16), slot_lengths)
    convolved = (
        jnp.einsum("ufk,ck->ufc", framed, conv_weight, preferred_element_type=jnp.float32)
        + conv_bias
    )
    active = jax.nn.gelu(layer_norm(convolved, conv_gain, conv_shift), approximate=False)
    live = live_of(slot_lengths, frame_total)
    frames = jnp.where(live[..., None], active, 0.0).astype(jnp.bfloat16)
    frames = frames.reshape(MICRO * rows, frames.shape[2])
    normed_frames = layer_norm(frames.astype(jnp.float32), feat_gain, feat_shift).astype(
        jnp.bfloat16
    )
    entering = (product(normed_frames, proj_weight) + proj_bias).astype(jnp.bfloat16)
    entering = entering.reshape(MICRO, rows, columns)

    owner = lax.broadcasted_iota(jnp.int32, (rows, rows), 0) // frame_total
    column = lax.broadcasted_iota(jnp.int32, (rows, rows), 1) // frame_total
    maskings = jnp.where((owner == column)[None] & live.reshape(MICRO, 1, rows), 1.0, 0.0)
    gain = norm_gain.reshape(group, 1, columns)
    shift = norm_shift.reshape(group, 1, columns)
    query, key, value = (
        weight.reshape(group, columns, HEAD_DIM)
        for weight in (query_weight, key_weight, value_weight)
    )
    out_part = out_weight.reshape(group // 2, 2 * HEAD_DIM, columns)

    vmem = pl.BlockSpec(memory_space=pltpu.VMEM)
    mixing = pl.pallas_call(
        mixing_kernel,
        out_shape=jax.ShapeDtypeStruct((rows, HEAD_DIM), jnp.bfloat16),
        in_specs=[vmem] * 7,
        out_specs=vmem,
        compiler_params=pltpu.CompilerParams(vmem_limit_bytes=24 * 2**20),
    )
    leaving = pl.pallas_call(
        leaving_kernel,
        out_shape=jax.ShapeDtypeStruct((rows, columns), jnp.bfloat16),
        in_specs=[vmem] * 4,
        out_specs=vmem,
        compiler_params=pltpu.CompilerParams(vmem_limit_bytes=24 * 2**20),
    )

    def to_all(block, axes, size):
        copies = jnp.broadcast_to(block[None], (size,) + block.shape)
        return lax.all_to_all(copies, axes, 0, 0, tiled=True)

    def attend(current, masking):
        chip_blocks = to_all(current, "y", chips)
        blocks = lax.all_gather(chip_blocks, "core", axis=1, tiled=False)
        blocks = blocks.reshape(group, rows, columns)
        mixture = mixing(blocks, gain, shift, query, key, value, masking)
        mixed = to_all(mixture, ("y", "core"), group)
        return leaving(mixed, current, out_part, out_bias)

    def gradients_of():
        own_lengths = lax.dynamic_slice_in_dim(lengths[0], chip * CORES + core, 1, 0)
        own_framed = framed_of(wave[0], own_lengths).astype(jnp.float32)
        own_live = live_of(own_lengths, frame_total)

        def frontend_at(weight, bias, gain, shift):
            return frontend(weight, bias, gain, shift, own_framed, own_live)

        _, pullback = jax.vjp(
            frontend_at, conv_weight.astype(jnp.float32), conv_bias, conv_gain, conv_shift
        )
        partial = pullback(feat_grad[0].astype(jnp.float32))
        packed = jnp.concatenate(
            [partial[0].T, partial[1][None], partial[2][None], partial[3][None]], axis=0
        )
        packed = jnp.pad(packed, ((0, 16 - packed.shape[0]), (0, 0)))
        return lax.psum(lax.psum(lax.psum(packed, "core"), "dp"), "y")

    late = section >= sections // 2
    packed = lax.cond(
        late, gradients_of, lambda: jnp.zeros((16, conv_bias.shape[0]), jnp.float32)
    )
    entering, packed = lax.optimization_barrier((entering, packed))

    def advance(tick, state):
        previous, outputs = state
        arrived = lax.ppermute(previous, "section", [(s, s + 1) for s in range(sections - 1)])
        piece = tick - section
        slot = jnp.clip(piece, 0, MICRO - 1)

        def work():
            fresh = lax.dynamic_index_in_dim(entering, slot, 0, keepdims=False)
            current = jnp.where(section == 0, fresh, arrived)
            masking = lax.dynamic_index_in_dim(maskings, slot, 0, keepdims=False)
            result = attend(current, masking)
            return (result, lax.dynamic_update_index_in_dim(outputs, result, slot, 0))

        return lax.cond(
            (piece >= 0) & (piece < MICRO), work, lambda: (previous, outputs)
        )

    start = (
        jnp.zeros((rows, columns), jnp.bfloat16),
        jnp.zeros((MICRO, rows, columns), jnp.bfloat16),
    )
    _, outputs = lax.fori_loop(0, sections + MICRO - 1, advance, start)
    outputs, packed = lax.optimization_barrier((outputs, packed))
    packed = lax.cond(late, lambda: packed, gradients_of)
    return (
        outputs[None, None],
        packed[:KERNEL].T,
        packed[KERNEL],
        packed[KERNEL + 1],
        packed[KERNEL + 2],
    )


def solution(mesh):
    sizes = dict(mesh.shape)
    split = Mesh(
        mesh.devices.reshape(
            sizes["section"], sizes["seq"] // CORES, CORES, sizes["dp"]
        ),
        ("section", "y", "core", "dp"),
    )
    seq = ("y", "core")
    return jax.shard_map(
        on_device,
        mesh=split,
        in_specs=(
            P("dp", seq, None),
            P("dp", None),
            P("dp", None),
            P(),
            P(),
            P(),
            P(),
            P(),
            P(),
            P(None, seq),
            P(seq),
            P("section", None),
            P("section", None),
            P("section", None, seq),
            P("section", None, seq),
            P("section", None, seq),
            P("section", None, seq),
            P("section", seq),
            P("dp", seq, None, None),
        ),
        out_specs=(P("section", "dp", None, None, seq), P(), P(), P(), P()),
        check_vma=False,
    )
```

```python
import jax
import jax.numpy as jnp
from jax import lax
from jax.experimental import pallas as pl
from jax.experimental.pallas import tpu as pltpu
from jax.sharding import Mesh, PartitionSpec as P

HEAD_DIM = 128
KERNEL = 10
STRIDE = 5
MICRO = 2
CORES = 2


def layer_norm(values, gain, shift):
    average = jnp.mean(values, axis=-1, keepdims=True)
    centered = values - average
    spread = jnp.mean(centered * centered, axis=-1, keepdims=True)
    return centered * lax.rsqrt(spread + 1e-05) * gain + shift


def frame_counts(lengths):
    return (lengths - KERNEL) // STRIDE + 1


def framed_of(wave, lengths):
    owners, samples = wave.shape
    positions = lax.broadcasted_iota(jnp.int32, wave.shape, 1)
    cleaned = jnp.where(positions < lengths[:, None], wave, jnp.zeros_like(wave))
    blocks = cleaned.reshape(owners, samples // STRIDE, STRIDE)
    after = jnp.concatenate([blocks[:, 1:], jnp.zeros_like(blocks[:, :1])], axis=1)
    return jnp.concatenate([blocks, after], axis=2)


def live_of(lengths, frame_total):
    counts = frame_counts(lengths)
    return lax.broadcasted_iota(jnp.int32, (lengths.shape[0], frame_total), 1) < counts[:, None]


def frontend(weight, bias, gain, shift, framed, live):
    convolved = (
        jnp.einsum("...fk,ck->...fc", framed, weight, precision=lax.Precision.HIGHEST) + bias
    )
    active = jax.nn.gelu(layer_norm(convolved, gain, shift), approximate=False)
    return jnp.where(live[..., None], active, jnp.zeros_like(active))


def product(left, right):
    return jnp.dot(left, right, preferred_element_type=jnp.float32)


def mixing_kernel(place, rows_ref, gain, shift, query, key, value, masking, out):
    rows, model = rows_ref.shape
    width = 2 * HEAD_DIM
    spans = [slice(at, at + width) for at in range(0, model, width)]
    total = jnp.zeros((rows, 1), jnp.float32)
    for span in spans:
        total += jnp.sum(rows_ref[:, span].astype(jnp.float32), axis=-1, keepdims=True)
    average = total / model
    spread = jnp.zeros_like(average)
    for span in spans:
        centered = rows_ref[:, span].astype(jnp.float32) - average
        spread += jnp.sum(centered * centered, axis=-1, keepdims=True)
    scale = lax.rsqrt(spread / model + 1e-05)
    both = jnp.zeros((rows, 2 * HEAD_DIM), jnp.float32)
    values = jnp.zeros((rows, HEAD_DIM), jnp.float32)
    for span in spans:
        centered = rows_ref[:, span].astype(jnp.float32) - average
        normed = (centered * scale * gain[:, span] + shift[:, span]).astype(jnp.bfloat16)
        both += product(normed, jnp.concatenate([query[span], key[span]], axis=1))
        values += product(normed, value[span])
    queries = (both[:, :HEAD_DIM] * HEAD_DIM ** (-0.5)).astype(jnp.bfloat16)
    key_rows = both[:, HEAD_DIM:].astype(jnp.bfloat16)
    scores = lax.dot_general(
        queries, key_rows, (((1,), (1,)), ((), ())), preferred_element_type=jnp.float32
    )
    scores = jnp.where(masking[place[0]] > 0, scores, -jnp.inf)
    raised = jnp.exp(scores - jnp.max(scores, axis=-1, keepdims=True))
    attention = (raised / jnp.sum(raised, axis=-1, keepdims=True)).astype(jnp.bfloat16)
    mixture = product(attention, values.astype(jnp.bfloat16)).astype(jnp.bfloat16)
    out[...] = jnp.broadcast_to(mixture[None], out.shape)


def leaving_kernel(place, mixed, current, weights, bias, _, out, outputs):
    total = current[...].astype(jnp.float32) + bias[...]
    for i in range(0, mixed.shape[0], 2):
        pair = jnp.concatenate([mixed[i], mixed[i + 1]], axis=1)
        total += product(pair, weights[i // 2])
    result = total.astype(jnp.bfloat16)
    out[...] = result
    outputs[place[0]] = result


def on_device(
    wave,
    lengths,
    assign,
    conv_weight,
    conv_bias,
    conv_gain,
    conv_shift,
    feat_gain,
    feat_shift,
    proj_weight,
    proj_bias,
    norm_gain,
    norm_shift,
    query_weight,
    key_weight,
    value_weight,
    out_weight,
    out_bias,
    feat_grad,
):
    section, chip, core = (lax.axis_index(name) for name in ("section", "y", "core"))
    sections, chips = lax.axis_size("section"), lax.axis_size("y")
    group = chips * CORES
    samples = wave.shape[2]
    frame_total = samples // STRIDE
    batch_size = lengths.shape[1]
    utts = batch_size // MICRO
    rows = utts * frame_total
    columns = proj_weight.shape[1]

    waves = lax.all_gather(wave[0].astype(jnp.float32), ("y", "core"), axis=0, tiled=True)
    slots = lax.broadcasted_iota(jnp.int32, (batch_size, batch_size), 1)
    chosen = assign[0][:, None] == slots
    slot_lengths = jnp.sum(jnp.where(chosen, lengths[0][:, None], 0), axis=0)
    slot_waves = jnp.sum(jnp.where(chosen[:, :, None], waves[:, None], 0.0), axis=0)
    framed = framed_of(slot_waves.astype(jnp.bfloat16), slot_lengths)
    convolved = (
        jnp.einsum("ufk,ck->ufc", framed, conv_weight, preferred_element_type=jnp.float32)
        + conv_bias
    )
    active = jax.nn.gelu(layer_norm(convolved, conv_gain, conv_shift), approximate=False)
    live = live_of(slot_lengths, frame_total)
    frames = jnp.where(live[..., None], active, 0.0).astype(jnp.bfloat16)
    frames = frames.reshape(MICRO * rows, frames.shape[2])
    normed_frames = layer_norm(frames.astype(jnp.float32), feat_gain, feat_shift).astype(
        jnp.bfloat16
    )
    entering = (product(normed_frames, proj_weight) + proj_bias).astype(jnp.bfloat16)
    entering = entering.reshape(MICRO, rows, columns)

    owner = lax.broadcasted_iota(jnp.int32, (rows, rows), 0) // frame_total
    column = lax.broadcasted_iota(jnp.int32, (rows, rows), 1) // frame_total
    maskings = jnp.where((owner == column)[None] & live.reshape(MICRO, 1, rows), 1.0, 0.0)
    out_part = out_weight.reshape(group // 2, 2 * HEAD_DIM, columns)

    vmem = pl.BlockSpec(memory_space=pltpu.VMEM)
    smem = pl.BlockSpec(memory_space=pltpu.SMEM)
    mixing = pl.pallas_call(
        mixing_kernel,
        out_shape=jax.ShapeDtypeStruct((group, rows, HEAD_DIM), jnp.bfloat16),
        in_specs=[smem] + [vmem] * 7,
        out_specs=vmem,
        compiler_params=pltpu.CompilerParams(vmem_limit_bytes=24 * 2**20),
    )
    leaving = pl.pallas_call(
        leaving_kernel,
        out_shape=(
            jax.ShapeDtypeStruct((rows, columns), jnp.bfloat16),
            jax.ShapeDtypeStruct((MICRO, rows, columns), jnp.bfloat16),
        ),
        in_specs=[smem] + [vmem] * 5,
        out_specs=(vmem, vmem),
        input_output_aliases={5: 1},
        compiler_params=pltpu.CompilerParams(vmem_limit_bytes=24 * 2**20),
    )

    def attend(current, slot, outputs):
        place = slot.reshape(1)
        whole = lax.all_gather(current, ("y", "core"), axis=1, tiled=True)
        copies = mixing(
            place,
            whole,
            norm_gain,
            norm_shift,
            query_weight[0],
            key_weight[0],
            value_weight[0],
            maskings,
        )
        mixed = lax.all_to_all(copies, ("y", "core"), 0, 0, tiled=True)
        return leaving(place, mixed, current, out_part, out_bias, outputs)

    def gradients_of():
        own_lengths = lax.dynamic_slice_in_dim(lengths[0], chip * CORES + core, 1, 0)
        own_framed = framed_of(wave[0], own_lengths).astype(jnp.float32)
        own_live = live_of(own_lengths, frame_total)

        def frontend_at(weight, bias, gain, shift):
            return frontend(weight, bias, gain, shift, own_framed, own_live)

        _, pullback = jax.vjp(
            frontend_at, conv_weight.astype(jnp.float32), conv_bias, conv_gain, conv_shift
        )
        partial = pullback(feat_grad[0].astype(jnp.float32))
        packed = jnp.concatenate(
            [partial[0].T, partial[1][None], partial[2][None], partial[3][None]], axis=0
        )
        packed = jnp.pad(packed, ((0, 16 - packed.shape[0]), (0, 0)))
        return lax.psum(lax.psum(lax.psum(packed, "core"), "dp"), "y")

    late = section >= sections // 2
    packed = lax.cond(
        late, gradients_of, lambda: jnp.zeros((16, conv_bias.shape[0]), jnp.float32)
    )
    entering, packed = lax.optimization_barrier((entering, packed))

    def advance(tick, state):
        previous, outputs = state
        arrived = lax.ppermute(previous, "section", [(s, s + 1) for s in range(sections - 1)])
        piece = tick - section
        slot = jnp.clip(piece, 0, MICRO - 1)

        def work():
            fresh = lax.dynamic_index_in_dim(entering, slot, 0, keepdims=False)
            current = jnp.where(section == 0, fresh, arrived)
            return tuple(attend(current, slot, outputs))

        return lax.cond(
            (piece >= 0) & (piece < MICRO), work, lambda: (previous, outputs)
        )

    start = (
        jnp.zeros((rows, columns), jnp.bfloat16),
        jnp.zeros((MICRO, rows, columns), jnp.bfloat16),
    )
    _, outputs = lax.fori_loop(0, sections + MICRO - 1, advance, start)
    outputs, packed = lax.optimization_barrier((outputs, packed))
    packed = lax.cond(late, lambda: packed, gradients_of)
    return (
        outputs[None, None],
        packed[:KERNEL].T,
        packed[KERNEL],
        packed[KERNEL + 1],
        packed[KERNEL + 2],
    )


def solution(mesh):
    sizes = dict(mesh.shape)
    split = Mesh(
        mesh.devices.reshape(
            sizes["section"], sizes["seq"] // CORES, CORES, sizes["dp"]
        ),
        ("section", "y", "core", "dp"),
    )
    seq = ("y", "core")
    return jax.shard_map(
        on_device,
        mesh=split,
        in_specs=(
            P("dp", seq, None),
            P("dp", None),
            P("dp", None),
            P(),
            P(),
            P(),
            P(),
            P(),
            P(),
            P(None, seq),
            P(seq),
            P("section", None),
            P("section", None),
            P("section", None, seq),
            P("section", None, seq),
            P("section", None, seq),
            P("section", None, seq),
            P("section", seq),
            P("dp", seq, None, None),
        ),
        out_specs=(P("section", "dp", None, None, seq), P(), P(), P(), P()),
        check_vma=False,
    )
```

```python
import functools

import jax
import jax.numpy as jnp
from jax import lax
from jax.experimental import pallas as pl
from jax.experimental.pallas import tpu as pltpu
from jax.sharding import Mesh, PartitionSpec as P

HEAD_DIM = 128
KERNEL = 10
STRIDE = 5
MICRO = 2
CORES = 2


def layer_norm(values, gain, shift):
    average = jnp.mean(values, axis=-1, keepdims=True)
    centered = values - average
    spread = jnp.mean(centered * centered, axis=-1, keepdims=True)
    return centered * lax.rsqrt(spread + 1e-05) * gain + shift


def frame_counts(lengths):
    return (lengths - KERNEL) // STRIDE + 1


def framed_of(wave, lengths):
    owners, samples = wave.shape
    positions = lax.broadcasted_iota(jnp.int32, wave.shape, 1)
    cleaned = jnp.where(positions < lengths[:, None], wave, jnp.zeros_like(wave))
    blocks = cleaned.reshape(owners, samples // STRIDE, STRIDE)
    after = jnp.concatenate([blocks[:, 1:], jnp.zeros_like(blocks[:, :1])], axis=1)
    return jnp.concatenate([blocks, after], axis=2)


def live_of(lengths, frame_total):
    counts = frame_counts(lengths)
    return lax.broadcasted_iota(jnp.int32, (lengths.shape[0], frame_total), 1) < counts[:, None]


def frontend(weight, bias, gain, shift, framed, live):
    convolved = (
        jnp.einsum("...fk,ck->...fc", framed, weight, precision=lax.Precision.HIGHEST) + bias
    )
    active = jax.nn.gelu(layer_norm(convolved, gain, shift), approximate=False)
    return jnp.where(live[..., None], active, jnp.zeros_like(active))


def product(left, right):
    return jnp.dot(left, right, preferred_element_type=jnp.float32)


def mixing_kernel(frame_total, place, rows_ref, gain, shift, query, key, value, live, out):
    rows, model = rows_ref.shape
    width = 2 * HEAD_DIM
    spans = [slice(at, at + width) for at in range(0, model, width)]
    total = jnp.zeros((rows, width), jnp.float32)
    for span in spans:
        total += rows_ref[:, span].astype(jnp.float32)
    average = jnp.sum(total, axis=-1, keepdims=True) / model
    total = jnp.zeros((rows, width), jnp.float32)
    for span in spans:
        centered = rows_ref[:, span].astype(jnp.float32) - average
        total += centered * centered
    spread = jnp.sum(total, axis=-1, keepdims=True)
    scale = lax.rsqrt(spread / model + 1e-05)
    both = jnp.zeros((rows, 2 * HEAD_DIM), jnp.float32)
    values = jnp.zeros((rows, HEAD_DIM), jnp.float32)
    for span in spans:
        centered = rows_ref[:, span].astype(jnp.float32) - average
        normed = (centered * scale * gain[:, span] + shift[:, span]).astype(jnp.bfloat16)
        both += product(normed, jnp.concatenate([query[span], key[span]], axis=1))
        values += product(normed, value[span])
    queries = (both[:, :HEAD_DIM] * HEAD_DIM ** (-0.5)).astype(jnp.bfloat16)
    key_rows = both[:, HEAD_DIM:].astype(jnp.bfloat16)
    scores = lax.dot_general(
        queries, key_rows, (((1,), (1,)), ((), ())), preferred_element_type=jnp.float32
    )
    owner = lax.broadcasted_iota(jnp.int32, (rows, rows), 0) // frame_total
    column = lax.broadcasted_iota(jnp.int32, (rows, rows), 1) // frame_total
    scores = jnp.where((owner == column) & (live[place[0]] > 0), scores, -jnp.inf)
    raised = jnp.exp(scores - jnp.max(scores, axis=-1, keepdims=True))
    attention = (raised / jnp.sum(raised, axis=-1, keepdims=True)).astype(jnp.bfloat16)
    mixture = product(attention, values.astype(jnp.bfloat16)).astype(jnp.bfloat16)
    out[...] = jnp.broadcast_to(mixture[None], out.shape)


def leaving_kernel(place, mixed, current, weights, bias, _, out, outputs):
    total = current[...].astype(jnp.float32) + bias[...]
    for i in range(mixed.shape[1]):
        pair = jnp.concatenate([mixed[0, i], mixed[1, i]], axis=1)
        total += product(pair, weights[i])
    result = total.astype(jnp.bfloat16)
    out[...] = result
    outputs[place[0]] = result


def on_device(
    wave,
    lengths,
    assign,
    conv_weight,
    conv_bias,
    conv_gain,
    conv_shift,
    feat_gain,
    feat_shift,
    proj_weight,
    proj_bias,
    norm_gain,
    norm_shift,
    query_weight,
    key_weight,
    value_weight,
    out_weight,
    out_bias,
    feat_grad,
):
    section, chip, core = (lax.axis_index(name) for name in ("section", "y", "core"))
    sections, chips = lax.axis_size("section"), lax.axis_size("y")
    group = chips * CORES
    samples = wave.shape[2]
    frame_total = samples // STRIDE
    batch_size = lengths.shape[1]
    utts = batch_size // MICRO
    rows = utts * frame_total
    columns = proj_weight.shape[1]

    waves = lax.all_gather(wave[0].astype(jnp.float32), ("y", "core"), axis=0, tiled=True)
    slots = lax.broadcasted_iota(jnp.int32, (batch_size, batch_size), 1)
    chosen = assign[0][:, None] == slots
    slot_lengths = jnp.sum(jnp.where(chosen, lengths[0][:, None], 0), axis=0)
    slot_waves = jnp.sum(jnp.where(chosen[:, :, None], waves[:, None], 0.0), axis=0)
    framed = framed_of(slot_waves.astype(jnp.bfloat16), slot_lengths)
    convolved = (
        jnp.einsum("ufk,ck->ufc", framed, conv_weight, preferred_element_type=jnp.float32)
        + conv_bias
    )
    active = jax.nn.gelu(layer_norm(convolved, conv_gain, conv_shift), approximate=False)
    live = live_of(slot_lengths, frame_total)
    frames = jnp.where(live[..., None], active, 0.0).astype(jnp.bfloat16)
    frames = frames.reshape(MICRO * rows, frames.shape[2])
    normed_frames = layer_norm(frames.astype(jnp.float32), feat_gain, feat_shift).astype(
        jnp.bfloat16
    )
    entering = (product(normed_frames, proj_weight) + proj_bias).astype(jnp.bfloat16)
    entering = entering.reshape(MICRO, rows, columns)

    live_keys = live.reshape(MICRO, 1, rows).astype(jnp.float32)
    out_part = out_weight.reshape(group // 2, 2 * HEAD_DIM, columns)

    vmem = pl.BlockSpec(memory_space=pltpu.VMEM)
    smem = pl.BlockSpec(memory_space=pltpu.SMEM)
    mixing = pl.pallas_call(
        functools.partial(mixing_kernel, frame_total),
        out_shape=jax.ShapeDtypeStruct((chips, rows, HEAD_DIM), jnp.bfloat16),
        in_specs=[smem] + [vmem] * 7,
        out_specs=vmem,
        compiler_params=pltpu.CompilerParams(vmem_limit_bytes=24 * 2**20),
    )
    leaving = pl.pallas_call(
        leaving_kernel,
        out_shape=(
            jax.ShapeDtypeStruct((rows, columns), jnp.bfloat16),
            jax.ShapeDtypeStruct((MICRO, rows, columns), jnp.bfloat16),
        ),
        in_specs=[smem] + [vmem] * 5,
        out_specs=(vmem, vmem),
        input_output_aliases={5: 1},
        compiler_params=pltpu.CompilerParams(vmem_limit_bytes=24 * 2**20),
    )

    def attend(current, slot, outputs):
        place = slot.reshape(1)
        whole = lax.all_gather(current, ("y", "core"), axis=1, tiled=True)
        copies = mixing(
            place,
            whole,
            norm_gain,
            norm_shift,
            query_weight[0],
            key_weight[0],
            value_weight[0],
            live_keys,
        )
        chip_mixed = lax.all_to_all(copies, "y", 0, 0, tiled=True)
        mixed = lax.all_gather(chip_mixed, "core", axis=0, tiled=False)
        return leaving(place, mixed, current, out_part, out_bias, outputs)

    def gradients_of():
        own_lengths = lax.dynamic_slice_in_dim(lengths[0], chip * CORES + core, 1, 0)
        own_framed = framed_of(wave[0], own_lengths).astype(jnp.float32)
        own_live = live_of(own_lengths, frame_total)

        def frontend_at(weight, bias, gain, shift):
            return frontend(weight, bias, gain, shift, own_framed, own_live)

        _, pullback = jax.vjp(
            frontend_at, conv_weight.astype(jnp.float32), conv_bias, conv_gain, conv_shift
        )
        partial = pullback(feat_grad[0].astype(jnp.float32))
        packed = jnp.concatenate(
            [partial[0].T, partial[1][None], partial[2][None], partial[3][None]], axis=0
        )
        packed = jnp.pad(packed, ((0, 16 - packed.shape[0]), (0, 0)))
        return lax.psum(lax.psum(lax.psum(packed, "core"), "dp"), "y")

    late = section >= sections // 2
    packed = lax.cond(
        late, gradients_of, lambda: jnp.zeros((16, conv_bias.shape[0]), jnp.float32)
    )
    entering, packed = lax.optimization_barrier((entering, packed))

    def advance(tick, state):
        previous, outputs = state
        arrived = lax.ppermute(previous, "section", [(s, s + 1) for s in range(sections - 1)])
        piece = tick - section
        slot = jnp.clip(piece, 0, MICRO - 1)

        def work():
            fresh = lax.dynamic_index_in_dim(entering, slot, 0, keepdims=False)
            current = jnp.where(section == 0, fresh, arrived)
            return tuple(attend(current, slot, outputs))

        return lax.cond(
            (piece >= 0) & (piece < MICRO), work, lambda: (previous, outputs)
        )

    start = (
        jnp.zeros((rows, columns), jnp.bfloat16),
        jnp.zeros((MICRO, rows, columns), jnp.bfloat16),
    )
    _, outputs = lax.fori_loop(0, sections + MICRO - 1, advance, start)
    outputs, packed = lax.optimization_barrier((outputs, packed))
    packed = lax.cond(late, lambda: packed, gradients_of)
    return (
        outputs[None, None],
        packed[:KERNEL].T,
        packed[KERNEL],
        packed[KERNEL + 1],
        packed[KERNEL + 2],
    )


def solution(mesh):
    sizes = dict(mesh.shape)
    split = Mesh(
        mesh.devices.reshape(
            sizes["section"], sizes["seq"] // CORES, CORES, sizes["dp"]
        ),
        ("section", "y", "core", "dp"),
    )
    seq = ("y", "core")
    return jax.shard_map(
        on_device,
        mesh=split,
        in_specs=(
            P("dp", seq, None),
            P("dp", None),
            P("dp", None),
            P(),
            P(),
            P(),
            P(),
            P(),
            P(),
            P(None, seq),
            P(seq),
            P("section", None),
            P("section", None),
            P("section", None, seq),
            P("section", None, seq),
            P("section", None, seq),
            P("section", None, seq),
            P("section", seq),
            P("dp", seq, None, None),
        ),
        out_specs=(P("section", "dp", None, None, seq), P(), P(), P(), P()),
        check_vma=False,
    )
```

```python
import jax
import jax.numpy as jnp
from jax import lax
from jax.experimental import pallas as pl
from jax.experimental.pallas import tpu as pltpu
from jax.sharding import Mesh, PartitionSpec as P

HEAD_DIM = 128
KERNEL = 10
STRIDE = 5
MICRO = 2
CORES = 2


def layer_norm(values, gain, shift):
    average = jnp.mean(values, axis=-1, keepdims=True)
    centered = values - average
    spread = jnp.mean(centered * centered, axis=-1, keepdims=True)
    return centered * lax.rsqrt(spread + 1e-05) * gain + shift


def frame_counts(lengths):
    return (lengths - KERNEL) // STRIDE + 1


def framed_of(wave, lengths):
    owners, samples = wave.shape
    positions = lax.broadcasted_iota(jnp.int32, wave.shape, 1)
    cleaned = jnp.where(positions < lengths[:, None], wave, jnp.zeros_like(wave))
    blocks = cleaned.reshape(owners, samples // STRIDE, STRIDE)
    after = jnp.concatenate([blocks[:, 1:], jnp.zeros_like(blocks[:, :1])], axis=1)
    return jnp.concatenate([blocks, after], axis=2)


def live_of(lengths, frame_total):
    counts = frame_counts(lengths)
    return lax.broadcasted_iota(jnp.int32, (lengths.shape[0], frame_total), 1) < counts[:, None]


def frontend(weight, bias, gain, shift, framed, live):
    convolved = (
        jnp.einsum("...fk,ck->...fc", framed, weight, precision=lax.Precision.HIGHEST) + bias
    )
    active = jax.nn.gelu(layer_norm(convolved, gain, shift), approximate=False)
    return jnp.where(live[..., None], active, jnp.zeros_like(active))


def product(left, right):
    return jnp.dot(left, right, preferred_element_type=jnp.float32)


def mixing_kernel(rows_ref, gain, shift, query, key, value, masking, out):
    rows, model = rows_ref.shape
    parts, width = query.shape[0], query.shape[1]
    spans = [slice(i * width, (i + 1) * width) for i in range(parts)]
    total = jnp.zeros((rows, width), jnp.float32)
    for span in spans:
        total += rows_ref[:, span].astype(jnp.float32)
    average = jnp.sum(total, axis=-1, keepdims=True) / model
    total = jnp.zeros((rows, width), jnp.float32)
    for span in spans:
        centered = rows_ref[:, span].astype(jnp.float32) - average
        total += centered * centered
    scale = lax.rsqrt(jnp.sum(total, axis=-1, keepdims=True) / model + 1e-05)
    both = jnp.zeros((rows, 2 * HEAD_DIM), jnp.float32)
    values = jnp.zeros((rows, HEAD_DIM), jnp.float32)
    for i, span in enumerate(spans):
        centered = rows_ref[:, span].astype(jnp.float32) - average
        normed = (centered * scale * gain[i] + shift[i]).astype(jnp.bfloat16)
        both += product(normed, jnp.concatenate([query[i], key[i]], axis=1))
        values += product(normed, value[i])
    queries = (both[:, :HEAD_DIM] * HEAD_DIM ** (-0.5)).astype(jnp.bfloat16)
    key_rows = both[:, HEAD_DIM:].astype(jnp.bfloat16)
    scores = lax.dot_general(
        queries, key_rows, (((1,), (1,)), ((), ())), preferred_element_type=jnp.float32
    )
    scores = jnp.where(masking[...] > 0, scores, -jnp.inf)
    raised = jnp.exp(scores - jnp.max(scores, axis=-1, keepdims=True))
    attention = (raised / jnp.sum(raised, axis=-1, keepdims=True)).astype(jnp.bfloat16)
    out[...] = product(attention, values.astype(jnp.bfloat16)).astype(jnp.bfloat16)


def leaving_kernel(place, mixed, current, weights, bias, _, out, outputs):
    total = current[...].astype(jnp.float32) + bias[...]
    for i in range(0, mixed.shape[0], 2):
        pair = jnp.concatenate([mixed[i], mixed[i + 1]], axis=1)
        total += product(pair, weights[i // 2])
    result = total.astype(jnp.bfloat16)
    out[...] = result
    outputs[place[0]] = result


def on_device(
    wave,
    lengths,
    assign,
    conv_weight,
    conv_bias,
    conv_gain,
    conv_shift,
    feat_gain,
    feat_shift,
    proj_weight,
    proj_bias,
    norm_gain,
    norm_shift,
    query_weight,
    key_weight,
    value_weight,
    out_weight,
    out_bias,
    feat_grad,
):
    section, chip, core = (lax.axis_index(name) for name in ("section", "y", "core"))
    sections, chips = lax.axis_size("section"), lax.axis_size("y")
    group = chips * CORES
    samples = wave.shape[2]
    frame_total = samples // STRIDE
    batch_size = lengths.shape[1]
    utts = batch_size // MICRO
    rows = utts * frame_total
    columns = proj_weight.shape[1]

    waves = lax.all_gather(wave[0].astype(jnp.float32), ("y", "core"), axis=0, tiled=True)
    slots = lax.broadcasted_iota(jnp.int32, (batch_size, batch_size), 1)
    chosen = assign[0][:, None] == slots
    slot_lengths = jnp.sum(jnp.where(chosen, lengths[0][:, None], 0), axis=0)
    slot_waves = jnp.sum(jnp.where(chosen[:, :, None], waves[:, None], 0.0), axis=0)
    framed = framed_of(slot_waves.astype(jnp.bfloat16), slot_lengths)
    convolved = (
        jnp.einsum("ufk,ck->ufc", framed, conv_weight, preferred_element_type=jnp.float32)
        + conv_bias
    )
    active = jax.nn.gelu(layer_norm(convolved, conv_gain, conv_shift), approximate=False)
    live = live_of(slot_lengths, frame_total)
    frames = jnp.where(live[..., None], active, 0.0).astype(jnp.bfloat16)
    frames = frames.reshape(MICRO * rows, frames.shape[2])
    normed_frames = layer_norm(frames.astype(jnp.float32), feat_gain, feat_shift).astype(
        jnp.bfloat16
    )
    entering = (product(normed_frames, proj_weight) + proj_bias).astype(jnp.bfloat16)
    entering = entering.reshape(MICRO, rows, columns)

    owner = lax.broadcasted_iota(jnp.int32, (rows, rows), 0) // frame_total
    column = lax.broadcasted_iota(jnp.int32, (rows, rows), 1) // frame_total
    maskings = jnp.where((owner == column)[None] & live.reshape(MICRO, 1, rows), 1.0, 0.0)
    gain = norm_gain.reshape(group, 1, columns)
    shift = norm_shift.reshape(group, 1, columns)
    query, key, value = (
        weight.reshape(group, columns, HEAD_DIM)
        for weight in (query_weight, key_weight, value_weight)
    )
    out_part = out_weight.reshape(group // 2, 2 * HEAD_DIM, columns)

    vmem = pl.BlockSpec(memory_space=pltpu.VMEM)
    smem = pl.BlockSpec(memory_space=pltpu.SMEM)
    mixing = pl.pallas_call(
        mixing_kernel,
        out_shape=jax.ShapeDtypeStruct((rows, HEAD_DIM), jnp.bfloat16),
        in_specs=[vmem] * 7,
        out_specs=vmem,
        compiler_params=pltpu.CompilerParams(vmem_limit_bytes=24 * 2**20),
    )
    leaving = pl.pallas_call(
        leaving_kernel,
        out_shape=(
            jax.ShapeDtypeStruct((rows, columns), jnp.bfloat16),
            jax.ShapeDtypeStruct((MICRO, rows, columns), jnp.bfloat16),
        ),
        in_specs=[smem] + [vmem] * 5,
        out_specs=(vmem, vmem),
        input_output_aliases={5: 1},
        compiler_params=pltpu.CompilerParams(vmem_limit_bytes=24 * 2**20),
    )

    def attend(current, slot, outputs):
        place = slot.reshape(1)
        whole = lax.all_gather(current, ("y", "core"), axis=1, tiled=True)
        masking = lax.dynamic_index_in_dim(maskings, slot, 0, keepdims=False)
        mixture = mixing(whole, gain, shift, query, key, value, masking)
        copies = jnp.broadcast_to(mixture[None], (group,) + mixture.shape)
        mixed = lax.all_to_all(copies, ("y", "core"), 0, 0, tiled=True)
        return leaving(place, mixed, current, out_part, out_bias, outputs)

    def gradients_of():
        own_lengths = lax.dynamic_slice_in_dim(lengths[0], chip * CORES + core, 1, 0)
        own_framed = framed_of(wave[0], own_lengths).astype(jnp.float32)
        own_live = live_of(own_lengths, frame_total)

        def frontend_at(weight, bias, gain, shift):
            return frontend(weight, bias, gain, shift, own_framed, own_live)

        _, pullback = jax.vjp(
            frontend_at, conv_weight.astype(jnp.float32), conv_bias, conv_gain, conv_shift
        )
        partial = pullback(feat_grad[0].astype(jnp.float32))
        packed = jnp.concatenate(
            [partial[0].T, partial[1][None], partial[2][None], partial[3][None]], axis=0
        )
        packed = jnp.pad(packed, ((0, 16 - packed.shape[0]), (0, 0)))
        return lax.psum(lax.psum(lax.psum(packed, "core"), "dp"), "y")

    late = section >= sections // 2
    packed = lax.cond(
        late, gradients_of, lambda: jnp.zeros((16, conv_bias.shape[0]), jnp.float32)
    )
    entering, packed = lax.optimization_barrier((entering, packed))

    def advance(tick, state):
        previous, outputs = state
        arrived = lax.ppermute(previous, "section", [(s, s + 1) for s in range(sections - 1)])
        piece = tick - section
        slot = jnp.clip(piece, 0, MICRO - 1)

        def work():
            fresh = lax.dynamic_index_in_dim(entering, slot, 0, keepdims=False)
            current = jnp.where(section == 0, fresh, arrived)
            return tuple(attend(current, slot, outputs))

        return lax.cond(
            (piece >= 0) & (piece < MICRO), work, lambda: (previous, outputs)
        )

    start = (
        jnp.zeros((rows, columns), jnp.bfloat16),
        jnp.zeros((MICRO, rows, columns), jnp.bfloat16),
    )
    _, outputs = lax.fori_loop(0, sections + MICRO - 1, advance, start)
    outputs, packed = lax.optimization_barrier((outputs, packed))
    packed = lax.cond(late, lambda: packed, gradients_of)
    return (
        outputs[None, None],
        packed[:KERNEL].T,
        packed[KERNEL],
        packed[KERNEL + 1],
        packed[KERNEL + 2],
    )


def solution(mesh):
    sizes = dict(mesh.shape)
    split = Mesh(
        mesh.devices.reshape(
            sizes["section"], sizes["seq"] // CORES, CORES, sizes["dp"]
        ),
        ("section", "y", "core", "dp"),
    )
    seq = ("y", "core")
    return jax.shard_map(
        on_device,
        mesh=split,
        in_specs=(
            P("dp", seq, None),
            P("dp", None),
            P("dp", None),
            P(),
            P(),
            P(),
            P(),
            P(),
            P(),
            P(None, seq),
            P(seq),
            P("section", None),
            P("section", None),
            P("section", None, seq),
            P("section", None, seq),
            P("section", None, seq),
            P("section", None, seq),
            P("section", seq),
            P("dp", seq, None, None),
        ),
        out_specs=(P("section", "dp", None, None, seq), P(), P(), P(), P()),
        check_vma=False,
    )
```

```python
import jax
import jax.numpy as jnp
from jax import lax
from jax.experimental import pallas as pl
from jax.experimental.pallas import tpu as pltpu
from jax.sharding import Mesh, PartitionSpec as P

HEAD_DIM = 128
KERNEL = 10
STRIDE = 5
MICRO = 2
CORES = 2


def layer_norm(values, gain, shift):
    average = jnp.mean(values, axis=-1, keepdims=True)
    centered = values - average
    spread = jnp.mean(centered * centered, axis=-1, keepdims=True)
    return centered * lax.rsqrt(spread + 1e-05) * gain + shift


def frame_counts(lengths):
    return (lengths - KERNEL) // STRIDE + 1


def framed_of(wave, lengths):
    owners, samples = wave.shape
    positions = lax.broadcasted_iota(jnp.int32, wave.shape, 1)
    cleaned = jnp.where(positions < lengths[:, None], wave, jnp.zeros_like(wave))
    blocks = cleaned.reshape(owners, samples // STRIDE, STRIDE)
    after = jnp.concatenate([blocks[:, 1:], jnp.zeros_like(blocks[:, :1])], axis=1)
    return jnp.concatenate([blocks, after], axis=2)


def live_of(lengths, frame_total):
    counts = frame_counts(lengths)
    return lax.broadcasted_iota(jnp.int32, (lengths.shape[0], frame_total), 1) < counts[:, None]


def frontend(weight, bias, gain, shift, framed, live):
    convolved = (
        jnp.einsum("...fk,ck->...fc", framed, weight, precision=lax.Precision.HIGHEST) + bias
    )
    active = jax.nn.gelu(layer_norm(convolved, gain, shift), approximate=False)
    return jnp.where(live[..., None], active, jnp.zeros_like(active))


def product(left, right):
    return jnp.dot(left, right, preferred_element_type=jnp.float32)


def mixing_kernel(place, rows_ref, gain, shift, query, key, value, masking, out):
    rows, model = rows_ref.shape
    width = 2 * HEAD_DIM
    step = min(model, 4 * width)
    steps = model // step

    def parts_of(i):
        at = pl.multiple_of(i * step, step)
        return [
            rows_ref[:, pl.ds(pl.multiple_of(at + inner, width), width)].astype(jnp.float32)
            for inner in range(0, step, width)
        ]

    def add_up(i, total):
        for part in parts_of(i):
            total += part
        return total

    zeros = jnp.zeros((rows, width), jnp.float32)
    total = lax.fori_loop(0, steps, add_up, zeros)
    average = jnp.sum(total, axis=-1, keepdims=True) / model

    def add_squares(i, total):
        for part in parts_of(i):
            total += (part - average) * (part - average)
        return total

    total = lax.fori_loop(0, steps, add_squares, zeros)
    scale = lax.rsqrt(jnp.sum(total, axis=-1, keepdims=True) / model + 1e-05)

    def project(i, sums):
        span = pl.ds(pl.multiple_of(i * step, step), step)
        centered = rows_ref[:, span].astype(jnp.float32) - average
        normed = (centered * scale * gain[:, span] + shift[:, span]).astype(jnp.bfloat16)
        pair = jnp.concatenate([query[span, :], key[span, :]], axis=1)
        return (sums[0] + product(normed, pair), sums[1] + product(normed, value[span, :]))

    both, values = lax.fori_loop(
        0, steps, project, (zeros, jnp.zeros((rows, HEAD_DIM), jnp.float32))
    )
    queries = (both[:, :HEAD_DIM] * HEAD_DIM ** (-0.5)).astype(jnp.bfloat16)
    key_rows = both[:, HEAD_DIM:].astype(jnp.bfloat16)
    scores = lax.dot_general(
        queries, key_rows, (((1,), (1,)), ((), ())), preferred_element_type=jnp.float32
    )
    scores = jnp.where(masking[place[0]] > 0, scores, -jnp.inf)
    raised = jnp.exp(scores - jnp.max(scores, axis=-1, keepdims=True))
    attention = (raised / jnp.sum(raised, axis=-1, keepdims=True)).astype(jnp.bfloat16)
    mixture = product(attention, values.astype(jnp.bfloat16)).astype(jnp.bfloat16)
    out[...] = jnp.broadcast_to(mixture[None], out.shape)


def leaving_kernel(place, mixed, current, weights, bias, held, out, outputs):
    def add_heads(i, total):
        for inner in range(2):
            at = 2 * i + inner
            pair = jnp.concatenate([mixed[2 * at], mixed[2 * at + 1]], axis=1)
            total += product(pair, weights[at])
        return total

    start = current[...].astype(jnp.float32) + bias[...]
    total = lax.fori_loop(0, weights.shape[0] // 2, add_heads, start)
    result = total.astype(jnp.bfloat16)
    out[...] = result
    outputs[...] = held[...]
    outputs[place[0]] = result


def on_device(
    wave,
    lengths,
    assign,
    conv_weight,
    conv_bias,
    conv_gain,
    conv_shift,
    feat_gain,
    feat_shift,
    proj_weight,
    proj_bias,
    norm_gain,
    norm_shift,
    query_weight,
    key_weight,
    value_weight,
    out_weight,
    out_bias,
    feat_grad,
):
    section, chip, core = (lax.axis_index(name) for name in ("section", "y", "core"))
    sections, chips = lax.axis_size("section"), lax.axis_size("y")
    group = chips * CORES
    samples = wave.shape[2]
    frame_total = samples // STRIDE
    batch_size = lengths.shape[1]
    utts = batch_size // MICRO
    rows = utts * frame_total
    columns = proj_weight.shape[1]

    waves = lax.all_gather(wave[0].astype(jnp.float32), ("y", "core"), axis=0, tiled=True)
    slots = lax.broadcasted_iota(jnp.int32, (batch_size, batch_size), 1)
    chosen = assign[0][:, None] == slots
    slot_lengths = jnp.sum(jnp.where(chosen, lengths[0][:, None], 0), axis=0)
    slot_waves = jnp.sum(jnp.where(chosen[:, :, None], waves[:, None], 0.0), axis=0)
    framed = framed_of(slot_waves.astype(jnp.bfloat16), slot_lengths)
    convolved = (
        jnp.einsum("ufk,ck->ufc", framed, conv_weight, preferred_element_type=jnp.float32)
        + conv_bias
    )
    active = jax.nn.gelu(layer_norm(convolved, conv_gain, conv_shift), approximate=False)
    live = live_of(slot_lengths, frame_total)
    frames = jnp.where(live[..., None], active, 0.0).astype(jnp.bfloat16)
    frames = frames.reshape(MICRO * rows, frames.shape[2])
    normed_frames = layer_norm(frames.astype(jnp.float32), feat_gain, feat_shift).astype(
        jnp.bfloat16
    )
    entering = (product(normed_frames, proj_weight) + proj_bias).astype(jnp.bfloat16)
    entering = entering.reshape(MICRO, rows, columns)

    owner = lax.broadcasted_iota(jnp.int32, (rows, rows), 0) // frame_total
    column = lax.broadcasted_iota(jnp.int32, (rows, rows), 1) // frame_total
    maskings = jnp.where((owner == column)[None] & live.reshape(MICRO, 1, rows), 1.0, 0.0)
    out_part = out_weight.reshape(group // 2, 2 * HEAD_DIM, columns)

    vmem = pl.BlockSpec(memory_space=pltpu.VMEM)
    smem = pl.BlockSpec(memory_space=pltpu.SMEM)
    mixing = pl.pallas_call(
        mixing_kernel,
        out_shape=jax.ShapeDtypeStruct((group, rows, HEAD_DIM), jnp.bfloat16),
        in_specs=[smem] + [vmem] * 7,
        out_specs=vmem,
        compiler_params=pltpu.CompilerParams(vmem_limit_bytes=24 * 2**20),
    )
    leaving = pl.pallas_call(
        leaving_kernel,
        out_shape=(
            jax.ShapeDtypeStruct((rows, columns), jnp.bfloat16),
            jax.ShapeDtypeStruct((MICRO, rows, columns), jnp.bfloat16),
        ),
        in_specs=[smem] + [vmem] * 5,
        out_specs=(vmem, vmem),
        input_output_aliases={5: 1},
        compiler_params=pltpu.CompilerParams(vmem_limit_bytes=24 * 2**20),
    )

    def attend(current, slot, outputs):
        place = slot.reshape(1)
        whole = lax.all_gather(current, ("y", "core"), axis=1, tiled=True)
        copies = mixing(
            place,
            whole,
            norm_gain,
            norm_shift,
            query_weight[0],
            key_weight[0],
            value_weight[0],
            maskings,
        )
        mixed = lax.all_to_all(copies, ("y", "core"), 0, 0, tiled=True)
        return leaving(place, mixed, current, out_part, out_bias, outputs)

    def gradients_of():
        own_lengths = lax.dynamic_slice_in_dim(lengths[0], chip * CORES + core, 1, 0)
        own_framed = framed_of(wave[0], own_lengths).astype(jnp.float32)
        own_live = live_of(own_lengths, frame_total)

        def frontend_at(weight, bias, gain, shift):
            return frontend(weight, bias, gain, shift, own_framed, own_live)

        _, pullback = jax.vjp(
            frontend_at, conv_weight.astype(jnp.float32), conv_bias, conv_gain, conv_shift
        )
        partial = pullback(feat_grad[0].astype(jnp.float32))
        packed = jnp.concatenate(
            [partial[0].T, partial[1][None], partial[2][None], partial[3][None]], axis=0
        )
        packed = jnp.pad(packed, ((0, 16 - packed.shape[0]), (0, 0)))
        return lax.psum(lax.psum(lax.psum(packed, "core"), "dp"), "y")

    late = section >= sections // 2
    packed = lax.cond(
        late, gradients_of, lambda: jnp.zeros((16, conv_bias.shape[0]), jnp.float32)
    )
    entering, packed = lax.optimization_barrier((entering, packed))

    def advance(tick, state):
        previous, outputs = state
        arrived = lax.ppermute(previous, "section", [(s, s + 1) for s in range(sections - 1)])
        piece = tick - section
        slot = jnp.clip(piece, 0, MICRO - 1)

        def work():
            fresh = lax.dynamic_index_in_dim(entering, slot, 0, keepdims=False)
            current = jnp.where(section == 0, fresh, arrived)
            return tuple(attend(current, slot, outputs))

        return lax.cond(
            (piece >= 0) & (piece < MICRO), work, lambda: (previous, outputs)
        )

    start = (
        jnp.zeros((rows, columns), jnp.bfloat16),
        jnp.zeros((MICRO, rows, columns), jnp.bfloat16),
    )
    _, outputs = lax.fori_loop(0, sections + MICRO - 1, advance, start)
    outputs, packed = lax.optimization_barrier((outputs, packed))
    packed = lax.cond(late, lambda: packed, gradients_of)
    return (
        outputs[None, None],
        packed[:KERNEL].T,
        packed[KERNEL],
        packed[KERNEL + 1],
        packed[KERNEL + 2],
    )


def solution(mesh):
    sizes = dict(mesh.shape)
    split = Mesh(
        mesh.devices.reshape(
            sizes["section"], sizes["seq"] // CORES, CORES, sizes["dp"]
        ),
        ("section", "y", "core", "dp"),
    )
    seq = ("y", "core")
    return jax.shard_map(
        on_device,
        mesh=split,
        in_specs=(
            P("dp", seq, None),
            P("dp", None),
            P("dp", None),
            P(),
            P(),
            P(),
            P(),
            P(),
            P(),
            P(None, seq),
            P(seq),
            P("section", None),
            P("section", None),
            P("section", None, seq),
            P("section", None, seq),
            P("section", None, seq),
            P("section", None, seq),
            P("section", seq),
            P("dp", seq, None, None),
        ),
        out_specs=(P("section", "dp", None, None, seq), P(), P(), P(), P()),
        check_vma=False,
    )
```

```python
import jax
import jax.numpy as jnp
from jax import lax
from jax.experimental import pallas as pl
from jax.experimental.pallas import tpu as pltpu
from jax.sharding import Mesh, PartitionSpec as P

HEAD_DIM = 128
KERNEL = 10
STRIDE = 5
MICRO = 2
CORES = 2


def layer_norm(values, gain, shift):
    average = jnp.mean(values, axis=-1, keepdims=True)
    centered = values - average
    spread = jnp.mean(centered * centered, axis=-1, keepdims=True)
    return centered * lax.rsqrt(spread + 1e-05) * gain + shift


def frame_counts(lengths):
    return (lengths - KERNEL) // STRIDE + 1


def framed_of(wave, lengths):
    owners, samples = wave.shape
    positions = lax.broadcasted_iota(jnp.int32, wave.shape, 1)
    cleaned = jnp.where(positions < lengths[:, None], wave, jnp.zeros_like(wave))
    blocks = cleaned.reshape(owners, samples // STRIDE, STRIDE)
    after = jnp.concatenate([blocks[:, 1:], jnp.zeros_like(blocks[:, :1])], axis=1)
    return jnp.concatenate([blocks, after], axis=2)


def live_of(lengths, frame_total):
    counts = frame_counts(lengths)
    return lax.broadcasted_iota(jnp.int32, (lengths.shape[0], frame_total), 1) < counts[:, None]


def frontend(weight, bias, gain, shift, framed, live):
    convolved = (
        jnp.einsum("...fk,ck->...fc", framed, weight, precision=lax.Precision.HIGHEST) + bias
    )
    active = jax.nn.gelu(layer_norm(convolved, gain, shift), approximate=False)
    return jnp.where(live[..., None], active, jnp.zeros_like(active))


def product(left, right):
    return jnp.dot(left, right, preferred_element_type=jnp.float32)


def mixing_kernel(place, blocks, gain, shift, query, key, value, masking, out):
    parts, rows, width = blocks.shape
    total = jnp.zeros((rows, width), jnp.float32)
    for i in range(parts):
        total += blocks[i].astype(jnp.float32)
    average = jnp.sum(total, axis=-1, keepdims=True) / (parts * width)
    total = jnp.zeros((rows, width), jnp.float32)
    for i in range(parts):
        centered = blocks[i].astype(jnp.float32) - average
        total += centered * centered
    spread = jnp.sum(total, axis=-1, keepdims=True) / (parts * width)
    scale = lax.rsqrt(spread + 1e-05)
    both = jnp.zeros((rows, 2 * HEAD_DIM), jnp.float32)
    values = jnp.zeros((rows, HEAD_DIM), jnp.float32)
    for i in range(parts):
        centered = blocks[i].astype(jnp.float32) - average
        normed = (centered * scale * gain[i] + shift[i]).astype(jnp.bfloat16)
        both += product(normed, jnp.concatenate([query[i], key[i]], axis=1))
        values += product(normed, value[i])
    queries = (both[:, :HEAD_DIM] * HEAD_DIM ** (-0.5)).astype(jnp.bfloat16)
    key_rows = both[:, HEAD_DIM:].astype(jnp.bfloat16)
    scores = lax.dot_general(
        queries, key_rows, (((1,), (1,)), ((), ())), preferred_element_type=jnp.float32
    )
    scores = jnp.where(masking[place[0]] > 0, scores, -jnp.inf)
    raised = jnp.exp(scores - jnp.max(scores, axis=-1, keepdims=True))
    attention = (raised / jnp.sum(raised, axis=-1, keepdims=True)).astype(jnp.bfloat16)
    mixture = product(attention, values.astype(jnp.bfloat16)).astype(jnp.bfloat16)
    out[...] = jnp.broadcast_to(mixture[None], out.shape)


def leaving_kernel(place, mixed, current, weights, bias, held, out, outputs):
    total = current[...].astype(jnp.float32) + bias[...]
    for i in range(0, mixed.shape[0], 2):
        pair = jnp.concatenate([mixed[i], mixed[i + 1]], axis=1)
        total += product(pair, weights[i // 2])
    result = total.astype(jnp.bfloat16)
    out[...] = result
    outputs[...] = held[...]
    outputs[place[0]] = result


def on_device(
    wave,
    lengths,
    assign,
    conv_weight,
    conv_bias,
    conv_gain,
    conv_shift,
    feat_gain,
    feat_shift,
    proj_weight,
    proj_bias,
    norm_gain,
    norm_shift,
    query_weight,
    key_weight,
    value_weight,
    out_weight,
    out_bias,
    feat_grad,
):
    section, chip, core = (lax.axis_index(name) for name in ("section", "y", "core"))
    sections, chips = lax.axis_size("section"), lax.axis_size("y")
    group = chips * CORES
    samples = wave.shape[2]
    frame_total = samples // STRIDE
    batch_size = lengths.shape[1]
    utts = batch_size // MICRO
    rows = utts * frame_total
    columns = proj_weight.shape[1]

    waves = lax.all_gather(wave[0].astype(jnp.float32), ("y", "core"), axis=0, tiled=True)
    slots = lax.broadcasted_iota(jnp.int32, (batch_size, batch_size), 1)
    chosen = assign[0][:, None] == slots
    slot_lengths = jnp.sum(jnp.where(chosen, lengths[0][:, None], 0), axis=0)
    slot_waves = jnp.sum(jnp.where(chosen[:, :, None], waves[:, None], 0.0), axis=0)
    framed = framed_of(slot_waves.astype(jnp.bfloat16), slot_lengths)
    convolved = (
        jnp.einsum("ufk,ck->ufc", framed, conv_weight, preferred_element_type=jnp.float32)
        + conv_bias
    )
    active = jax.nn.gelu(layer_norm(convolved, conv_gain, conv_shift), approximate=False)
    live = live_of(slot_lengths, frame_total)
    frames = jnp.where(live[..., None], active, 0.0).astype(jnp.bfloat16)
    frames = frames.reshape(MICRO * rows, frames.shape[2])
    normed_frames = layer_norm(frames.astype(jnp.float32), feat_gain, feat_shift).astype(
        jnp.bfloat16
    )
    entering = (product(normed_frames, proj_weight) + proj_bias).astype(jnp.bfloat16)
    entering = entering.reshape(MICRO, rows, columns)

    owner = lax.broadcasted_iota(jnp.int32, (rows, rows), 0) // frame_total
    column = lax.broadcasted_iota(jnp.int32, (rows, rows), 1) // frame_total
    maskings = jnp.where((owner == column)[None] & live.reshape(MICRO, 1, rows), 1.0, 0.0)
    gain = norm_gain.reshape(group, 1, columns)
    shift = norm_shift.reshape(group, 1, columns)
    query, key, value = (
        weight.reshape(group, columns, HEAD_DIM)
        for weight in (query_weight, key_weight, value_weight)
    )
    out_part = out_weight.reshape(group // 2, 2 * HEAD_DIM, columns)

    vmem = pl.BlockSpec(memory_space=pltpu.VMEM)
    smem = pl.BlockSpec(memory_space=pltpu.SMEM)
    mixing = pl.pallas_call(
        mixing_kernel,
        out_shape=jax.ShapeDtypeStruct((group, rows, HEAD_DIM), jnp.bfloat16),
        in_specs=[smem] + [vmem] * 7,
        out_specs=vmem,
        compiler_params=pltpu.CompilerParams(vmem_limit_bytes=24 * 2**20),
    )
    leaving = pl.pallas_call(
        leaving_kernel,
        out_shape=(
            jax.ShapeDtypeStruct((rows, columns), jnp.bfloat16),
            jax.ShapeDtypeStruct((MICRO, rows, columns), jnp.bfloat16),
        ),
        in_specs=[smem] + [vmem] * 5,
        out_specs=(vmem, vmem),
        input_output_aliases={5: 1},
        compiler_params=pltpu.CompilerParams(vmem_limit_bytes=24 * 2**20),
    )

    def attend(current, slot, outputs):
        place = slot.reshape(1)
        whole = lax.all_gather(current, ("y", "core"), axis=0, tiled=False)
        copies = mixing(place, whole, gain, shift, query, key, value, maskings)
        mixed = lax.all_to_all(copies, ("y", "core"), 0, 0, tiled=True)
        return leaving(place, mixed, current, out_part, out_bias, outputs)

    def gradients_of():
        own_lengths = lax.dynamic_slice_in_dim(lengths[0], chip * CORES + core, 1, 0)
        own_framed = framed_of(wave[0], own_lengths).astype(jnp.float32)
        own_live = live_of(own_lengths, frame_total)

        def frontend_at(weight, bias, gain, shift):
            return frontend(weight, bias, gain, shift, own_framed, own_live)

        _, pullback = jax.vjp(
            frontend_at, conv_weight.astype(jnp.float32), conv_bias, conv_gain, conv_shift
        )
        partial = pullback(feat_grad[0].astype(jnp.float32))
        packed = jnp.concatenate(
            [partial[0].T, partial[1][None], partial[2][None], partial[3][None]], axis=0
        )
        packed = jnp.pad(packed, ((0, 16 - packed.shape[0]), (0, 0)))
        return lax.psum(lax.psum(lax.psum(packed, "core"), "dp"), "y")

    late = section >= sections // 2
    packed = lax.cond(
        late, gradients_of, lambda: jnp.zeros((16, conv_bias.shape[0]), jnp.float32)
    )
    entering, packed = lax.optimization_barrier((entering, packed))

    def advance(tick, state):
        previous, outputs = state
        arrived = lax.ppermute(previous, "section", [(s, s + 1) for s in range(sections - 1)])
        piece = tick - section
        slot = jnp.clip(piece, 0, MICRO - 1)

        def work():
            fresh = lax.dynamic_index_in_dim(entering, slot, 0, keepdims=False)
            current = jnp.where(section == 0, fresh, arrived)
            return tuple(attend(current, slot, outputs))

        return lax.cond(
            (piece >= 0) & (piece < MICRO), work, lambda: (previous, outputs)
        )

    start = (
        jnp.zeros((rows, columns), jnp.bfloat16),
        jnp.zeros((MICRO, rows, columns), jnp.bfloat16),
    )
    _, outputs = lax.fori_loop(0, sections + MICRO - 1, advance, start)
    outputs, packed = lax.optimization_barrier((outputs, packed))
    packed = lax.cond(late, lambda: packed, gradients_of)
    return (
        outputs[None, None],
        packed[:KERNEL].T,
        packed[KERNEL],
        packed[KERNEL + 1],
        packed[KERNEL + 2],
    )


def solution(mesh):
    sizes = dict(mesh.shape)
    split = Mesh(
        mesh.devices.reshape(
            sizes["section"], sizes["seq"] // CORES, CORES, sizes["dp"]
        ),
        ("section", "y", "core", "dp"),
    )
    seq = ("y", "core")
    return jax.shard_map(
        on_device,
        mesh=split,
        in_specs=(
            P("dp", seq, None),
            P("dp", None),
            P("dp", None),
            P(),
            P(),
            P(),
            P(),
            P(),
            P(),
            P(None, seq),
            P(seq),
            P("section", None),
            P("section", None),
            P("section", None, seq),
            P("section", None, seq),
            P("section", None, seq),
            P("section", None, seq),
            P("section", seq),
            P("dp", seq, None, None),
        ),
        out_specs=(P("section", "dp", None, None, seq), P(), P(), P(), P()),
        check_vma=False,
    )
```

```python
import jax
import jax.numpy as jnp
from jax import lax
from jax.experimental import pallas as pl
from jax.experimental.pallas import tpu as pltpu
from jax.sharding import Mesh, PartitionSpec as P

HEAD_DIM = 128
KERNEL = 10
STRIDE = 5
MICRO = 2
CORES = 2


def layer_norm(values, gain, shift):
    average = jnp.mean(values, axis=-1, keepdims=True)
    centered = values - average
    spread = jnp.mean(centered * centered, axis=-1, keepdims=True)
    return centered * lax.rsqrt(spread + 1e-05) * gain + shift


def frame_counts(lengths):
    return (lengths - KERNEL) // STRIDE + 1


def framed_of(wave, lengths):
    owners, samples = wave.shape
    positions = lax.broadcasted_iota(jnp.int32, wave.shape, 1)
    cleaned = jnp.where(positions < lengths[:, None], wave, jnp.zeros_like(wave))
    blocks = cleaned.reshape(owners, samples // STRIDE, STRIDE)
    after = jnp.concatenate([blocks[:, 1:], jnp.zeros_like(blocks[:, :1])], axis=1)
    return jnp.concatenate([blocks, after], axis=2)


def live_of(lengths, frame_total):
    counts = frame_counts(lengths)
    return lax.broadcasted_iota(jnp.int32, (lengths.shape[0], frame_total), 1) < counts[:, None]


def frontend(weight, bias, gain, shift, framed, live):
    convolved = (
        jnp.einsum("...fk,ck->...fc", framed, weight, precision=lax.Precision.HIGHEST) + bias
    )
    active = jax.nn.gelu(layer_norm(convolved, gain, shift), approximate=False)
    return jnp.where(live[..., None], active, jnp.zeros_like(active))


def product(left, right):
    return jnp.dot(left, right, preferred_element_type=jnp.float32)


def mixing_kernel(place, blocks, gain, shift, query, key, value, masking, out):
    parts, rows, width = blocks.shape
    total = jnp.zeros((rows, 1), jnp.float32)
    for i in range(parts):
        total += jnp.sum(blocks[i].astype(jnp.float32), axis=-1, keepdims=True)
    average = total / (parts * width)
    spread = jnp.zeros_like(average)
    for i in range(parts):
        centered = blocks[i].astype(jnp.float32) - average
        spread += jnp.sum(centered * centered, axis=-1, keepdims=True)
    scale = lax.rsqrt(spread / (parts * width) + 1e-05)
    both = jnp.zeros((rows, 2 * HEAD_DIM), jnp.float32)
    values = jnp.zeros((rows, HEAD_DIM), jnp.float32)
    for i in range(parts):
        centered = blocks[i].astype(jnp.float32) - average
        normed = (centered * scale * gain[i] + shift[i]).astype(jnp.bfloat16)
        both += product(normed, jnp.concatenate([query[i], key[i]], axis=1))
        values += product(normed, value[i])
    queries = (both[:, :HEAD_DIM] * HEAD_DIM ** (-0.5)).astype(jnp.bfloat16)
    key_rows = both[:, HEAD_DIM:].astype(jnp.bfloat16)
    scores = lax.dot_general(
        queries, key_rows, (((1,), (1,)), ((), ())), preferred_element_type=jnp.float32
    )
    scores = jnp.where(masking[place[0]] > 0, scores, -jnp.inf)
    raised = jnp.exp(scores - jnp.max(scores, axis=-1, keepdims=True))
    attention = (raised / jnp.sum(raised, axis=-1, keepdims=True)).astype(jnp.bfloat16)
    mixture = product(attention, values.astype(jnp.bfloat16)).astype(jnp.bfloat16)
    out[...] = jnp.broadcast_to(mixture[None], out.shape)


def leaving_kernel(place, mixed, current, weights, bias, held, out, outputs):
    total = current[...].astype(jnp.float32) + bias[...]
    for i in range(0, mixed.shape[0], 2):
        pair = jnp.concatenate([mixed[i], mixed[i + 1]], axis=1)
        total += product(pair, weights[i // 2])
    result = total.astype(jnp.bfloat16)
    out[...] = result
    outputs[...] = held[...]
    outputs[place[0]] = result


def on_device(
    wave,
    lengths,
    assign,
    conv_weight,
    conv_bias,
    conv_gain,
    conv_shift,
    feat_gain,
    feat_shift,
    proj_weight,
    proj_bias,
    norm_gain,
    norm_shift,
    query_weight,
    key_weight,
    value_weight,
    out_weight,
    out_bias,
    feat_grad,
):
    section, chip, core = (lax.axis_index(name) for name in ("section", "y", "core"))
    sections, chips = lax.axis_size("section"), lax.axis_size("y")
    group = chips * CORES
    samples = wave.shape[2]
    frame_total = samples // STRIDE
    batch_size = lengths.shape[1]
    utts = batch_size // MICRO
    rows = utts * frame_total
    columns = proj_weight.shape[1]

    waves = lax.all_gather(wave[0].astype(jnp.float32), ("y", "core"), axis=0, tiled=True)
    slots = lax.broadcasted_iota(jnp.int32, (batch_size, batch_size), 1)
    chosen = assign[0][:, None] == slots
    slot_lengths = jnp.sum(jnp.where(chosen, lengths[0][:, None], 0), axis=0)
    slot_waves = jnp.sum(jnp.where(chosen[:, :, None], waves[:, None], 0.0), axis=0)
    framed = framed_of(slot_waves.astype(jnp.bfloat16), slot_lengths)
    convolved = (
        jnp.einsum("ufk,ck->ufc", framed, conv_weight, preferred_element_type=jnp.float32)
        + conv_bias
    )
    active = jax.nn.gelu(layer_norm(convolved, conv_gain, conv_shift), approximate=False)
    live = live_of(slot_lengths, frame_total)
    frames = jnp.where(live[..., None], active, 0.0).astype(jnp.bfloat16)
    frames = frames.reshape(MICRO * rows, frames.shape[2])
    normed_frames = layer_norm(frames.astype(jnp.float32), feat_gain, feat_shift).astype(
        jnp.bfloat16
    )
    entering = (product(normed_frames, proj_weight) + proj_bias).astype(jnp.bfloat16)
    entering = entering.reshape(MICRO, rows, columns)

    owner = lax.broadcasted_iota(jnp.int32, (rows, rows), 0) // frame_total
    column = lax.broadcasted_iota(jnp.int32, (rows, rows), 1) // frame_total
    maskings = jnp.where((owner == column)[None] & live.reshape(MICRO, 1, rows), 1.0, 0.0)
    gain = norm_gain.reshape(group, 1, columns)
    shift = norm_shift.reshape(group, 1, columns)
    query, key, value = (
        weight.reshape(group, columns, HEAD_DIM)
        for weight in (query_weight, key_weight, value_weight)
    )
    out_part = out_weight.reshape(group // 2, 2 * HEAD_DIM, columns)

    vmem = pl.BlockSpec(memory_space=pltpu.VMEM)
    smem = pl.BlockSpec(memory_space=pltpu.SMEM)
    mixing = pl.pallas_call(
        mixing_kernel,
        out_shape=jax.ShapeDtypeStruct((group, rows, HEAD_DIM), jnp.bfloat16),
        in_specs=[smem] + [vmem] * 7,
        out_specs=vmem,
        compiler_params=pltpu.CompilerParams(vmem_limit_bytes=24 * 2**20),
    )
    leaving = pl.pallas_call(
        leaving_kernel,
        out_shape=(
            jax.ShapeDtypeStruct((rows, columns), jnp.bfloat16),
            jax.ShapeDtypeStruct((MICRO, rows, columns), jnp.bfloat16),
        ),
        in_specs=[smem] + [vmem] * 5,
        out_specs=(vmem, vmem),
        input_output_aliases={5: 1},
        compiler_params=pltpu.CompilerParams(vmem_limit_bytes=24 * 2**20),
    )

    def attend(current, slot, outputs):
        place = slot.reshape(1)
        whole = lax.all_gather(current, ("y", "core"), axis=0, tiled=False)
        copies = mixing(place, whole, gain, shift, query, key, value, maskings)
        mixed = lax.all_to_all(copies, ("y", "core"), 0, 0, tiled=True)
        return leaving(place, mixed, current, out_part, out_bias, outputs)

    def gradients_of():
        own_lengths = lax.dynamic_slice_in_dim(lengths[0], chip * CORES + core, 1, 0)
        own_framed = framed_of(wave[0], own_lengths).astype(jnp.float32)
        own_live = live_of(own_lengths, frame_total)

        def frontend_at(weight, bias, gain, shift):
            return frontend(weight, bias, gain, shift, own_framed, own_live)

        _, pullback = jax.vjp(
            frontend_at, conv_weight.astype(jnp.float32), conv_bias, conv_gain, conv_shift
        )
        partial = pullback(feat_grad[0].astype(jnp.float32))
        packed = jnp.concatenate(
            [partial[0].T, partial[1][None], partial[2][None], partial[3][None]], axis=0
        )
        packed = jnp.pad(packed, ((0, 16 - packed.shape[0]), (0, 0)))
        return lax.psum(lax.psum(lax.psum(packed, "core"), "dp"), "y")

    late = section >= sections // 2
    packed = lax.cond(
        late, gradients_of, lambda: jnp.zeros((16, conv_bias.shape[0]), jnp.float32)
    )
    entering, packed = lax.optimization_barrier((entering, packed))

    def advance(tick, state):
        previous, outputs = state
        arrived = lax.ppermute(previous, "section", [(s, s + 1) for s in range(sections - 1)])
        piece = tick - section
        slot = jnp.clip(piece, 0, MICRO - 1)

        def work():
            fresh = lax.dynamic_index_in_dim(entering, slot, 0, keepdims=False)
            current = jnp.where(section == 0, fresh, arrived)
            return tuple(attend(current, slot, outputs))

        return lax.cond(
            (piece >= 0) & (piece < MICRO), work, lambda: (previous, outputs)
        )

    start = (
        jnp.zeros((rows, columns), jnp.bfloat16),
        jnp.zeros((MICRO, rows, columns), jnp.bfloat16),
    )
    _, outputs = lax.fori_loop(0, sections + MICRO - 1, advance, start)
    outputs, packed = lax.optimization_barrier((outputs, packed))
    packed = lax.cond(late, lambda: packed, gradients_of)
    return (
        outputs[None, None],
        packed[:KERNEL].T,
        packed[KERNEL],
        packed[KERNEL + 1],
        packed[KERNEL + 2],
    )


def solution(mesh):
    sizes = dict(mesh.shape)
    split = Mesh(
        mesh.devices.reshape(
            sizes["section"], sizes["seq"] // CORES, CORES, sizes["dp"]
        ),
        ("section", "y", "core", "dp"),
    )
    seq = ("y", "core")
    return jax.shard_map(
        on_device,
        mesh=split,
        in_specs=(
            P("dp", seq, None),
            P("dp", None),
            P("dp", None),
            P(),
            P(),
            P(),
            P(),
            P(),
            P(),
            P(None, seq),
            P(seq),
            P("section", None),
            P("section", None),
            P("section", None, seq),
            P("section", None, seq),
            P("section", None, seq),
            P("section", None, seq),
            P("section", seq),
            P("dp", seq, None, None),
        ),
        out_specs=(P("section", "dp", None, None, seq), P(), P(), P(), P()),
        check_vma=False,
    )
```

```python
import jax
import jax.numpy as jnp
from jax import lax
from jax.experimental import pallas as pl
from jax.experimental.pallas import tpu as pltpu
from jax.sharding import Mesh, PartitionSpec as P

HEAD_DIM = 128
KERNEL = 10
STRIDE = 5
MICRO = 2
CORES = 2


def layer_norm(values, gain, shift):
    average = jnp.mean(values, axis=-1, keepdims=True)
    centered = values - average
    spread = jnp.mean(centered * centered, axis=-1, keepdims=True)
    return centered * lax.rsqrt(spread + 1e-05) * gain + shift


def frame_counts(lengths):
    return (lengths - KERNEL) // STRIDE + 1


def framed_of(wave, lengths):
    owners, samples = wave.shape
    positions = lax.broadcasted_iota(jnp.int32, wave.shape, 1)
    cleaned = jnp.where(positions < lengths[:, None], wave, jnp.zeros_like(wave))
    blocks = cleaned.reshape(owners, samples // STRIDE, STRIDE)
    after = jnp.concatenate([blocks[:, 1:], jnp.zeros_like(blocks[:, :1])], axis=1)
    return jnp.concatenate([blocks, after], axis=2)


def live_of(lengths, frame_total):
    counts = frame_counts(lengths)
    return lax.broadcasted_iota(jnp.int32, (lengths.shape[0], frame_total), 1) < counts[:, None]


def frontend(weight, bias, gain, shift, framed, live):
    convolved = (
        jnp.einsum("...fk,ck->...fc", framed, weight, precision=lax.Precision.HIGHEST) + bias
    )
    active = jax.nn.gelu(layer_norm(convolved, gain, shift), approximate=False)
    return jnp.where(live[..., None], active, jnp.zeros_like(active))


def product(left, right):
    return jnp.dot(left, right, preferred_element_type=jnp.float32)


def mixing_kernel(place, blocks, gain, shift, query, key, value, masking, out):
    parts, rows, width = blocks.shape
    total = jnp.zeros((rows, width), jnp.float32)
    for i in range(parts):
        total += blocks[i].astype(jnp.float32)
    average = jnp.sum(total, axis=-1, keepdims=True) / (parts * width)
    total = jnp.zeros((rows, width), jnp.float32)
    for i in range(parts):
        centered = blocks[i].astype(jnp.float32) - average
        total += centered * centered
    spread = jnp.sum(total, axis=-1, keepdims=True) / (parts * width)
    scale = lax.rsqrt(spread + 1e-05)
    both = jnp.zeros((rows, 2 * HEAD_DIM), jnp.float32)
    values = jnp.zeros((rows, HEAD_DIM), jnp.float32)
    for i in range(parts):
        centered = blocks[i].astype(jnp.float32) - average
        normed = (centered * scale * gain[i] + shift[i]).astype(jnp.bfloat16)
        both += product(normed, jnp.concatenate([query[i], key[i]], axis=1))
        values += product(normed, value[i])
    queries = (both[:, :HEAD_DIM] * HEAD_DIM ** (-0.5)).astype(jnp.bfloat16)
    key_rows = both[:, HEAD_DIM:].astype(jnp.bfloat16)
    scores = lax.dot_general(
        queries, key_rows, (((1,), (1,)), ((), ())), preferred_element_type=jnp.float32
    )
    scores = jnp.where(masking[place[0]] > 0, scores, -jnp.inf)
    raised = jnp.exp(scores - jnp.max(scores, axis=-1, keepdims=True))
    attention = (raised / jnp.sum(raised, axis=-1, keepdims=True)).astype(jnp.bfloat16)
    mixture = product(attention, values.astype(jnp.bfloat16)).astype(jnp.bfloat16)
    out[...] = mixture


def leaving_kernel(place, mixed, current, weights, bias, held, out, outputs):
    total = current[...].astype(jnp.float32) + bias[...]
    for i in range(0, mixed.shape[0], 2):
        pair = jnp.concatenate([mixed[i], mixed[i + 1]], axis=1)
        total += product(pair, weights[i // 2])
    result = total.astype(jnp.bfloat16)
    out[...] = result
    outputs[...] = held[...]
    outputs[place[0]] = result


def on_device(
    wave,
    lengths,
    assign,
    conv_weight,
    conv_bias,
    conv_gain,
    conv_shift,
    feat_gain,
    feat_shift,
    proj_weight,
    proj_bias,
    norm_gain,
    norm_shift,
    query_weight,
    key_weight,
    value_weight,
    out_weight,
    out_bias,
    feat_grad,
):
    section, chip, core = (lax.axis_index(name) for name in ("section", "y", "core"))
    sections, chips = lax.axis_size("section"), lax.axis_size("y")
    group = chips * CORES
    samples = wave.shape[2]
    frame_total = samples // STRIDE
    batch_size = lengths.shape[1]
    utts = batch_size // MICRO
    rows = utts * frame_total
    columns = proj_weight.shape[1]

    waves = lax.all_gather(wave[0].astype(jnp.float32), ("y", "core"), axis=0, tiled=True)
    slots = lax.broadcasted_iota(jnp.int32, (batch_size, batch_size), 1)
    chosen = assign[0][:, None] == slots
    slot_lengths = jnp.sum(jnp.where(chosen, lengths[0][:, None], 0), axis=0)
    slot_waves = jnp.sum(jnp.where(chosen[:, :, None], waves[:, None], 0.0), axis=0)
    framed = framed_of(slot_waves.astype(jnp.bfloat16), slot_lengths)
    convolved = (
        jnp.einsum("ufk,ck->ufc", framed, conv_weight, preferred_element_type=jnp.float32)
        + conv_bias
    )
    active = jax.nn.gelu(layer_norm(convolved, conv_gain, conv_shift), approximate=False)
    live = live_of(slot_lengths, frame_total)
    frames = jnp.where(live[..., None], active, 0.0).astype(jnp.bfloat16)
    frames = frames.reshape(MICRO * rows, frames.shape[2])
    normed_frames = layer_norm(frames.astype(jnp.float32), feat_gain, feat_shift).astype(
        jnp.bfloat16
    )
    entering = (product(normed_frames, proj_weight) + proj_bias).astype(jnp.bfloat16)
    entering = entering.reshape(MICRO, rows, columns)

    owner = lax.broadcasted_iota(jnp.int32, (rows, rows), 0) // frame_total
    column = lax.broadcasted_iota(jnp.int32, (rows, rows), 1) // frame_total
    maskings = jnp.where((owner == column)[None] & live.reshape(MICRO, 1, rows), 1.0, 0.0)
    gain = norm_gain.reshape(group, 1, columns)
    shift = norm_shift.reshape(group, 1, columns)
    query, key, value = (
        weight.reshape(group, columns, HEAD_DIM)
        for weight in (query_weight, key_weight, value_weight)
    )
    out_part = out_weight.reshape(group // 2, 2 * HEAD_DIM, columns)

    vmem = pl.BlockSpec(memory_space=pltpu.VMEM)
    smem = pl.BlockSpec(memory_space=pltpu.SMEM)
    mixing = pl.pallas_call(
        mixing_kernel,
        out_shape=jax.ShapeDtypeStruct((rows, HEAD_DIM), jnp.bfloat16),
        in_specs=[smem] + [vmem] * 7,
        out_specs=vmem,
        compiler_params=pltpu.CompilerParams(vmem_limit_bytes=24 * 2**20),
    )
    leaving = pl.pallas_call(
        leaving_kernel,
        out_shape=(
            jax.ShapeDtypeStruct((rows, columns), jnp.bfloat16),
            jax.ShapeDtypeStruct((MICRO, rows, columns), jnp.bfloat16),
        ),
        in_specs=[smem] + [vmem] * 5,
        out_specs=(vmem, vmem),
        input_output_aliases={5: 1},
        compiler_params=pltpu.CompilerParams(vmem_limit_bytes=24 * 2**20),
    )

    def attend(current, slot, outputs):
        place = slot.reshape(1)
        whole = lax.all_gather(current, ("y", "core"), axis=0, tiled=False)
        mixture = mixing(place, whole, gain, shift, query, key, value, maskings)
        mixed = lax.all_gather(mixture, ("y", "core"), axis=0, tiled=False)
        return leaving(place, mixed, current, out_part, out_bias, outputs)

    def gradients_of():
        own_lengths = lax.dynamic_slice_in_dim(lengths[0], chip * CORES + core, 1, 0)
        own_framed = framed_of(wave[0], own_lengths).astype(jnp.float32)
        own_live = live_of(own_lengths, frame_total)

        def frontend_at(weight, bias, gain, shift):
            return frontend(weight, bias, gain, shift, own_framed, own_live)

        _, pullback = jax.vjp(
            frontend_at, conv_weight.astype(jnp.float32), conv_bias, conv_gain, conv_shift
        )
        partial = pullback(feat_grad[0].astype(jnp.float32))
        packed = jnp.concatenate(
            [partial[0].T, partial[1][None], partial[2][None], partial[3][None]], axis=0
        )
        packed = jnp.pad(packed, ((0, 16 - packed.shape[0]), (0, 0)))
        return lax.psum(lax.psum(lax.psum(packed, "core"), "dp"), "y")

    late = section >= sections // 2
    packed = lax.cond(
        late, gradients_of, lambda: jnp.zeros((16, conv_bias.shape[0]), jnp.float32)
    )
    entering, packed = lax.optimization_barrier((entering, packed))

    def advance(tick, state):
        previous, outputs = state
        arrived = lax.ppermute(previous, "section", [(s, s + 1) for s in range(sections - 1)])
        piece = tick - section
        slot = jnp.clip(piece, 0, MICRO - 1)

        def work():
            fresh = lax.dynamic_index_in_dim(entering, slot, 0, keepdims=False)
            current = jnp.where(section == 0, fresh, arrived)
            return tuple(attend(current, slot, outputs))

        return lax.cond(
            (piece >= 0) & (piece < MICRO), work, lambda: (previous, outputs)
        )

    start = (
        jnp.zeros((rows, columns), jnp.bfloat16),
        jnp.zeros((MICRO, rows, columns), jnp.bfloat16),
    )
    _, outputs = lax.fori_loop(0, sections + MICRO - 1, advance, start)
    outputs, packed = lax.optimization_barrier((outputs, packed))
    packed = lax.cond(late, lambda: packed, gradients_of)
    return (
        outputs[None, None],
        packed[:KERNEL].T,
        packed[KERNEL],
        packed[KERNEL + 1],
        packed[KERNEL + 2],
    )


def solution(mesh):
    sizes = dict(mesh.shape)
    split = Mesh(
        mesh.devices.reshape(
            sizes["section"], sizes["seq"] // CORES, CORES, sizes["dp"]
        ),
        ("section", "y", "core", "dp"),
    )
    seq = ("y", "core")
    return jax.shard_map(
        on_device,
        mesh=split,
        in_specs=(
            P("dp", seq, None),
            P("dp", None),
            P("dp", None),
            P(),
            P(),
            P(),
            P(),
            P(),
            P(),
            P(None, seq),
            P(seq),
            P("section", None),
            P("section", None),
            P("section", None, seq),
            P("section", None, seq),
            P("section", None, seq),
            P("section", None, seq),
            P("section", seq),
            P("dp", seq, None, None),
        ),
        out_specs=(P("section", "dp", None, None, seq), P(), P(), P(), P()),
        check_vma=False,
    )
```
